256 devices in a mesh: prompt: 16 (over z, x_lo), sample: 16 (over x_hi, y, core).
Axes of the slice: x: 4 (x_hi: 2, x_lo: 2; x = x_hi * 2 + x_lo), y: 4, z: 8, core: 2. Of those that a mesh axis runs over, the one named last changes fastest.
Arguments:
- queries: bfloat16 [16, 16, 32, 2048], P('prompt', 'sample'), may hold values from -12 to 12
- out_grad: bfloat16 [16, 16, 32, 2048], P('prompt', 'sample'), may hold values from -6 to 6
- advantage: float32 [16, 16], P('prompt', 'sample'), may hold values from -4 to 4
- comp_len: int32 [16, 16], P('prompt', 'sample'), may hold values from 1 to 32
- prefix_keys: bfloat16 [16, 2048, 512], P('prompt', 'sample'), may hold values from -4 to 4
- prefix_values: bfloat16 [16, 2048, 512], P('prompt', 'sample'), may hold values from -6 to 6
- own_keys: bfloat16 [16, 16, 32, 512], P('prompt', 'sample'), may hold values from -10 to 10
- own_values: bfloat16 [16, 16, 32, 512], P('prompt', 'sample'), may hold values from -6 to 6
- prompt_len: int32 [16], P('prompt'), may hold values from 512 to 2048
Outputs:
- query_grad: bfloat16 [16, 16, 32, 2048], P('prompt', 'sample')
- prefix_key_grad: bfloat16 [16, 2048, 512], P('prompt', 'sample')
- prefix_value_grad: bfloat16 [16, 2048, 512], P('prompt', 'sample')
- own_key_grad: bfloat16 [16, 16, 32, 512], P('prompt', 'sample')
- own_value_grad: bfloat16 [16, 16, 32, 512], P('prompt', 'sample')
The draws below stay inside these ranges and needn't reach their ends.
All inputs are finite; a program needn't handle non-finite values.
Results may differ from the reference program's by a relative error of at most 0.0075.
Values may be sent and summed in bfloat16 or wider, within the bound.
No kernel may reach another device: no remote copies, remote signals or barrier semaphores. Data moves between devices by JAX's collectives and lax.ppermute only.
A program may use at most 64 MiB of HBM per device.

```python
import math
import jax
import jax.numpy as jnp
from jax import lax

H = 16
KVH = 4
HD = 128
SLICE = 32
PROMPTS = 16
GROUP = 16
S = 2048


def key_table(key, pinned_size):
    normal_base = jax.random.normal(jax.random.fold_in(key, 11), (PROMPTS, S, KVH * HD), jnp.float32)
    table = jnp.clip(normal_base, -4.0, 4.0)
    flips = jax.random.bernoulli(jax.random.fold_in(key, 13), 0.5, (PROMPTS, KVH * HD))
    pinned = pinned_size * jnp.where(flips, 1.0, -1.0)
    places = lax.iota(jnp.int32, S)
    first_row = ((places == 1) & (pinned_size > 0.0))[None, :, None]
    second_row = ((places == 2) & (pinned_size > 0.0))[None, :, None]
    table = jnp.where(first_row, pinned[:, None, :], table)
    table = jnp.where(second_row, pinned[:, None, :] * 0.9921875, table)
    return table


def draw_prefix_keys(key, part):
    table = key_table(key, 0.0)
    return table.astype(jnp.bfloat16)


def draw_queries(key, part):
    key = jax.random.fold_in(key, 3)
    drawn = jnp.clip(jax.random.normal(key, (PROMPTS, GROUP, SLICE, H * HD), jnp.float32), -4.0, 4.0)
    return drawn.astype(jnp.bfloat16)


def draw_prompt_len(key, part):
    key = jax.random.fold_in(key, 7)
    lengths = jax.random.randint(key, (PROMPTS,), S // 4, S + 1)
    return lengths.at[0].set(S).astype(jnp.int32)


def draw_comp_len(key, part):
    key = jax.random.fold_in(key, 9)
    order = lax.iota(jnp.int32, PROMPTS * GROUP)
    ceiling = SLICE // 4 + (SLICE - SLICE // 4) * order // max(PROMPTS * GROUP - 1, 1)
    picked = jax.random.randint(key, (PROMPTS * GROUP,), 0, 1 << 20) % ceiling
    lengths = (1 + picked).at[0].set(1).at[PROMPTS * GROUP - 1].set(SLICE)
    return lengths.reshape(PROMPTS, GROUP).astype(jnp.int32)


def steps_of(own_key, shape, cuts, smallest, largest):
    level, own = 1.0, jax.random.fold_in(own_key, 6)
    for position, parts in cuts:
        heights = jnp.exp(jax.random.uniform(jax.random.fold_in(own, position), (parts,), jnp.float32, smallest / len(cuts), largest / len(cuts)))
        level = level * jnp.repeat(heights, shape[position] // parts).reshape([-1 if axis == position else 1 for axis in range(len(shape))])
    return level


def bell_draw(own_key, dims, width, bound, cuts=(), kind=jnp.bfloat16):
    values = jax.random.normal(own_key, dims, jnp.float32) * width
    if len(cuts) > 0:
        values = steps_of(own_key, dims, cuts, -0.22, 0.18) * values
    return jnp.clip(values, min=-bound, max=bound).astype(kind)


def setup_inputs(seed: int = 0) -> dict:
    key_list = jax.random.split(jax.random.key(seed), 10)
    queries = draw_queries(jax.random.fold_in(key_list[9], 71), 0)
    out_grad = bell_draw(key_list[1], (PROMPTS, GROUP, SLICE, H * HD), 1.0, 6.0, ((0, 16), (1, 16)))
    advantage = bell_draw(key_list[2], (PROMPTS, GROUP), 1.0, 4.0, ((0, 16), (1, 16)), jnp.float32)
    comp_len = draw_comp_len(jax.random.fold_in(key_list[9], 71), 0)
    prefix_keys = draw_prefix_keys(jax.random.fold_in(key_list[9], 71), 0)
    prefix_values = bell_draw(key_list[5], (PROMPTS, S, KVH * HD), 1.0, 6.0, ((0, 16), (1, 16)))
    own_keys = bell_draw(key_list[6], (PROMPTS, GROUP, SLICE, KVH * HD), 2.5, 10.0, ((0, 16), (1, 16)))
    own_values = bell_draw(key_list[7], (PROMPTS, GROUP, SLICE, KVH * HD), 1.0, 6.0, ((0, 16), (1, 16)))
    prompt_len = draw_prompt_len(jax.random.fold_in(key_list[9], 71), 0)
    return {"queries": queries, "out_grad": out_grad, "advantage": advantage, "comp_len": comp_len, "prefix_keys": prefix_keys, "prefix_values": prefix_values, "own_keys": own_keys, "own_values": own_values, "prompt_len": prompt_len}


MASKED = -1e+30

def to_half(values_in):
    return lax.optimization_barrier(values_in.astype(jnp.bfloat16)).astype(jnp.float32)

def one_prompt(packed):
    q_all, g_all, key_rows, value_rows, own_k, own_v, plen = packed
    group_size = H // KVH
    softmax_scale = 1.0 / math.sqrt(HD)
    key_ok = lax.iota(jnp.int32, S) < plen
    positions = lax.iota(jnp.int32, SLICE)
    causal = positions[None, :] <= positions[:, None]
    dq_list, dk_list, dv_list, dko_list, dvo_list = ([], [], [], [], [])
    for kv_group in range(KVH):
        start_col = kv_group * group_size * HD
        end_col = start_col + group_size * HD
        q_part = q_all[:, :, start_col:end_col].reshape(GROUP, SLICE, group_size, HD).astype(jnp.float32)
        g_part = g_all[:, :, start_col:end_col].reshape(GROUP, SLICE, group_size, HD).astype(jnp.float32)
        k_part = key_rows[:, kv_group * HD:(kv_group + 1) * HD].astype(jnp.float32)
        v_part = value_rows[:, kv_group * HD:(kv_group + 1) * HD].astype(jnp.float32)
        ko_part = own_k[:, :, kv_group * HD:(kv_group + 1) * HD].astype(jnp.float32)
        vo_part = own_v[:, :, kv_group * HD:(kv_group + 1) * HD].astype(jnp.float32)
        pre_scores = jnp.einsum('ctxd,jd->xctj', q_part, k_part) * softmax_scale
        pre_scores = jnp.where(key_ok, pre_scores, MASKED)
        own_scores = jnp.einsum('ctxd,cud->xctu', q_part, ko_part) * softmax_scale
        own_scores = jnp.where(causal[None, None], own_scores, MASKED)
        row_max = jnp.maximum(lax.optimization_barrier(jnp.max(pre_scores, axis=-1)), lax.optimization_barrier(jnp.max(own_scores, axis=-1)))
        pre_exp = jnp.exp(pre_scores - row_max[..., None])
        own_exp = jnp.exp(own_scores - row_max[..., None])
        row_sum = lax.optimization_barrier(jnp.sum(pre_exp, axis=-1)) + lax.optimization_barrier(jnp.sum(own_exp, axis=-1))
        pre_probs = pre_exp / row_sum[..., None]
        own_probs = own_exp / row_sum[..., None]
        pre_slopes = jnp.einsum('ctxd,jd->xctj', g_part, v_part)
        own_slopes = jnp.einsum('ctxd,cud->xctu', g_part, vo_part)
        row_mean = lax.optimization_barrier(jnp.sum(pre_probs * pre_slopes, axis=-1)) + lax.optimization_barrier(jnp.sum(own_probs * own_slopes, axis=-1))
        pre_dscore = to_half(pre_probs * (pre_slopes - row_mean[..., None]))
        own_dscore = to_half(own_probs * (own_slopes - row_mean[..., None]))
        dq_part = jnp.einsum('xctj,jd->ctxd', pre_dscore, k_part) + jnp.einsum('xctu,cud->ctxd', own_dscore, ko_part)
        dq_list.append((dq_part * softmax_scale).reshape(GROUP, SLICE, group_size * HD))
        dk_list.append(jnp.einsum('xctj,ctxd->jd', pre_dscore, q_part) * softmax_scale)
        dv_list.append(jnp.einsum('xctj,ctxd->jd', to_half(pre_probs), g_part))
        dko_list.append(jnp.einsum('xctu,ctxd->cud', own_dscore, q_part) * softmax_scale)
        dvo_list.append(jnp.einsum('xctu,ctxd->cud', to_half(own_probs), g_part))
    return (jnp.concatenate(dq_list, axis=-1), jnp.concatenate(dk_list, axis=-1), jnp.concatenate(dv_list, axis=-1), jnp.concatenate(dko_list, axis=-1), jnp.concatenate(dvo_list, axis=-1))

def reference(queries, out_grad, advantage, comp_len, prefix_keys, prefix_values, own_keys, own_values, prompt_len):
    positions = lax.iota(jnp.int32, SLICE)
    valid_mask = (positions[None, None, :] < comp_len[:, :, None]).astype(jnp.float32)
    token_weight = valid_mask * advantage[:, :, None]
    weighted = (out_grad.astype(jnp.float32) * token_weight[..., None]).astype(jnp.bfloat16)
    token_total = jnp.sum(comp_len.astype(jnp.float32))
    loss_scale = PROMPTS * GROUP * SLICE * math.sqrt(S) / (4.0 * token_total)
    grads = lax.map(one_prompt, (queries, weighted, prefix_keys, prefix_values, own_keys, own_values, prompt_len))
    return ((grads[0] * loss_scale).astype(jnp.bfloat16), (grads[1] * loss_scale).astype(jnp.bfloat16), (grads[2] * loss_scale).astype(jnp.bfloat16), (grads[3] * loss_scale).astype(jnp.bfloat16), (grads[4] * loss_scale).astype(jnp.bfloat16))
```

```python
import functools
import math

import jax
import jax.numpy as jnp
from jax import lax
from jax.experimental import pallas as pl
from jax.experimental.pallas import tpu as pltpu
from jax.sharding import PartitionSpec as P

HD = 128
MASKED = -1e30
VMEM_LIMIT = 24 * 1024 * 1024
NT = (((1,), (1,)), ((), ()))
NN = (((1,), (0,)), ((), ()))


def dot(a, b, dims):
    return lax.dot_general(a, b, dims, preferred_element_type=jnp.float32)


def pack_kernel(len_ref, adv_ref, q_ref, g_ref, out_ref):
    tokens, width = q_ref.shape
    heads = width // HD
    at = lax.broadcasted_iota(jnp.int32, (tokens, HD), 0)
    weight = jnp.where(at < len_ref[0], adv_ref[0], 0.0)
    for h in range(heads):
        cols = slice(h * HD, (h + 1) * HD)
        out_ref[h * tokens : (h + 1) * tokens, :] = q_ref[:, cols]
        out_ref[(heads + h) * tokens : (heads + h + 1) * tokens, :] = (
            g_ref[:, cols].astype(jnp.float32) * weight
        ).astype(jnp.bfloat16)


def rows_of(refs, start, size):
    return jnp.concatenate([r[start : start + size, :] for r in refs], axis=0)


def cols_of(refs, g):
    return jnp.concatenate([r[:, g * HD : (g + 1) * HD] for r in refs], axis=0)


def key_bias(info_ref, block):
    at = lax.broadcasted_iota(jnp.int32, (block, 1), 0)
    return jnp.concatenate(
        [
            jnp.where(at + info_ref[1 + k] * block < info_ref[0], 0.0, MASKED)
            for k in range(4)
        ],
        axis=0,
    )


def own_mask(tokens, rows):
    u = lax.broadcasted_iota(jnp.int32, (tokens, rows), 0)
    t = lax.broadcasted_iota(jnp.int32, (tokens, rows), 1) % tokens
    return u <= t


def stats_kernel(to_log2, info_ref, tot_ref, *refs):
    qg, ks, vs = refs[0:4], refs[4:8], refs[8:12]
    ok_ref, ov_ref, out_ref = refs[12:15]
    block = ks[0].shape[0]
    groups = ks[0].shape[1] // HD
    tokens = ok_ref.shape[0]
    all_rows = qg[0].shape[0] // 2
    rows = all_rows // groups
    bias = key_bias(info_ref, block)
    causal = own_mask(tokens, rows)
    out_ref[48:56, :] = jnp.zeros((8, HD), jnp.float32) + tot_ref[0]
    for g in range(groups):
        q = rows_of(qg, g * rows, rows)
        w = rows_of(qg, all_rows + g * rows, rows)
        score = dot(cols_of(ks, g), q, NT) * to_log2 + bias
        slope = dot(cols_of(vs, g), w, NT)
        own_cols = slice(g * HD, (g + 1) * HD)
        own_score = dot(ok_ref[:, own_cols], q[:rows], NT) * to_log2
        own_score = jnp.where(causal, own_score, MASKED)
        own_slope = dot(ov_ref[:, own_cols], w[:rows], NT)
        top = jnp.max(score, axis=0, keepdims=True)
        own_top = jnp.maximum(
            top[:, :rows], jnp.max(own_score, axis=0, keepdims=True)
        )
        top = jnp.concatenate([own_top, top[:, rows:]], axis=1)
        e = jnp.exp2(score - top)
        total = jnp.sum(e, axis=0, keepdims=True)
        mixed = jnp.sum(e * slope, axis=0, keepdims=True)
        own_e = jnp.exp2(own_score - own_top)
        own_total = jnp.sum(own_e, axis=0, keepdims=True)
        own_mixed = jnp.sum(own_e * own_slope, axis=0, keepdims=True)
        for s in range(4):
            lanes = slice(s * rows, (s + 1) * rows)
            at = s * 4 + g
            out_ref[at : at + 1, :] = top[:, lanes]
            extra = (own_total, own_mixed) if s == 0 else (0.0, 0.0)
            out_ref[16 + at : 17 + at, :] = total[:, lanes] + extra[0]
            out_ref[32 + at : 33 + at, :] = mixed[:, lanes] + extra[1]


def grads_kernel(to_log2, info_ref, *refs):
    qg, ks, vs = refs[0:4], refs[4:8], refs[8:12]
    ok_ref, ov_ref = refs[12:14]
    stats = refs[14:18]
    dq_own, dq_far, dq_sib, dkv_own = refs[18:22]
    dkv_out = refs[22:25]
    own_out, tot_out = refs[25:27]
    block = ks[0].shape[0]
    groups = ks[0].shape[1] // HD
    tokens = ok_ref.shape[0]
    all_rows = qg[0].shape[0] // 2
    rows = all_rows // groups
    bias = key_bias(info_ref, block)
    causal = own_mask(tokens, rows)
    shifts, means = [], []
    for s in range(4):
        tops = [stats[e][(s ^ e) * 4 : (s ^ e) * 4 + 4, :] for e in range(4)]
        top = functools.reduce(jnp.maximum, tops)
        total, mixed = 0.0, 0.0
        for e in range(4):
            factor = jnp.exp2(tops[e] - top)
            at = (s ^ e) * 4
            total += stats[e][16 + at : 20 + at, :] * factor
            mixed += stats[e][32 + at : 36 + at, :] * factor
        shifts.append(top + jnp.log2(total))
        means.append(mixed / total)
    shift = jnp.concatenate(shifts, axis=1)
    mean = jnp.concatenate(means, axis=1)
    count = sum(stats[e][48:56, :] for e in range(4))
    tot_out[...] = count
    high = jnp.floor(count * (1.0 / 256.0))
    marks = jnp.concatenate([high, count - high * 256.0], axis=0).astype(jnp.bfloat16)
    half = groups * block
    for ref in dkv_out:
        ref[2 * half : 2 * half + 16, :] = marks
    for g in range(groups):
        q = rows_of(qg, g * rows, rows)
        w = rows_of(qg, all_rows + g * rows, rows)
        k = cols_of(ks, g)
        sh, mn = shift[g : g + 1, :], mean[g : g + 1, :]
        score = dot(k, q, NT) * to_log2 + bias
        slope = dot(cols_of(vs, g), w, NT)
        p = jnp.exp2(score - sh)
        ds = (p * (slope - mn)).astype(jnp.bfloat16)
        dv = dot(p.astype(jnp.bfloat16), w, NN)
        dk = dot(ds, q, NN)
        dq = dot(k.T, ds, NN)
        own_cols = slice(g * HD, (g + 1) * HD)
        own_k = ok_ref[:, own_cols]
        own_score = dot(own_k, q[:rows], NT) * to_log2
        own_score = jnp.where(causal, own_score, MASKED)
        own_slope = dot(ov_ref[:, own_cols], w[:rows], NT)
        own_p = jnp.exp2(own_score - sh[:, :rows])
        own_ds = (own_p * (own_slope - mn[:, :rows])).astype(jnp.bfloat16)
        own_out[:tokens, own_cols] = dot(own_ds, q[:rows], NN)
        own_out[tokens:, own_cols] = dot(own_p.astype(jnp.bfloat16), w[:rows], NN)
        own_dq = dot(own_k.T, own_ds, NN)
        at = slice(g * HD, (g + 1) * HD)
        dq_own[at, :] = dq[:, :rows] + own_dq
        dq_far[at, :] = dq[:, 2 * rows : 3 * rows]
        dq_sib[at, :] = dq[:, rows : 2 * rows].astype(jnp.bfloat16)
        dq_sib[half_at(dq_sib, g), :] = dq[:, 3 * rows :].astype(jnp.bfloat16)
        here = slice(g * block, (g + 1) * block)
        there = slice(half + g * block, half + (g + 1) * block)
        dkv_own[here, :] = dk[:block]
        dkv_own[there, :] = dv[:block]
        for e in range(3):
            part = slice((e + 1) * block, (e + 2) * block)
            dkv_out[e][here, :] = dk[part].astype(jnp.bfloat16)
            dkv_out[e][there, :] = dv[part].astype(jnp.bfloat16)


def half_at(ref, g):
    half = ref.shape[0] // 2
    return slice(half + g * HD, half + (g + 1) * HD)


def finish_kernel(loss_top, softmax_scale, *refs):
    dq_own, dq_core, dq_x, dkv_own, r1, r2, r3, own_ref, tot_ref = refs[:9]
    q_out, k_out, v_out, ok_out, ov_out = refs[9:]
    block = k_out.shape[0]
    groups = k_out.shape[1] // HD
    tokens = ok_out.shape[0]
    per_group = q_out.shape[1] // HD // groups
    half = groups * block
    f32 = jnp.float32
    count = tot_ref[...]
    for r in (r1, r2, r3):
        marks = r[2 * half : 2 * half + 16, :].astype(f32)
        count = count + marks[:8] * 256.0 + marks[8:]
    scale = loss_top / count[:1, :]
    key_scale = scale * softmax_scale
    for g in range(groups):
        cols = slice(g * HD, (g + 1) * HD)
        dq = (
            dq_own[cols, :]
            + dq_core[cols, :].astype(f32)
            + dq_x[cols, :].astype(f32)
        ).T * key_scale
        for x in range(per_group):
            h = g * per_group + x
            q_out[:, h * HD : (h + 1) * HD] = dq[x * tokens : (x + 1) * tokens].astype(
                jnp.bfloat16
            )
        for out, start, by in ((k_out, 0, key_scale), (v_out, half, scale)):
            at = slice(start + g * block, start + (g + 1) * block)
            term = (dkv_own[at, :] + r1[at, :].astype(f32)) + (
                r2[at, :].astype(f32) + r3[at, :].astype(f32)
            )
            out[:, cols] = (term * by).astype(jnp.bfloat16)
        ok_out[:, cols] = (own_ref[:tokens, cols] * key_scale).astype(jnp.bfloat16)
        ov_out[:, cols] = (own_ref[tokens:, cols] * scale).astype(jnp.bfloat16)


def per_device(
    queries,
    out_grad,
    advantage,
    comp_len,
    prefix_keys,
    prefix_values,
    own_keys,
    own_values,
    prompt_len,
):
    samples = lax.axis_size("sample")
    prompts = lax.axis_size("prompt")
    tokens, width = queries.shape[2], queries.shape[3]
    block, kv_width = prefix_keys.shape[1], prefix_keys.shape[2]
    groups = kv_width // HD
    softmax_scale = 1.0 / math.sqrt(HD)
    to_log2 = softmax_scale * math.log2(math.e)
    loss_top = prompts * samples * tokens * math.sqrt(block * samples) / 4.0
    bf16, f32 = jnp.bfloat16, jnp.float32
    vmem = pl.BlockSpec(memory_space=pltpu.VMEM)
    smem = pl.BlockSpec(memory_space=pltpu.SMEM)
    params = pltpu.CompilerParams(vmem_limit_bytes=VMEM_LIMIT)
    shape = jax.ShapeDtypeStruct

    def swap(array, mask):
        return lax.ppermute(array, "sample", [(i, i ^ mask) for i in range(samples)])

    k0, v0 = prefix_keys[0], prefix_values[0]
    ks = [k0] + [swap(k0, 2 * e) for e in (1, 2, 3)]
    vs = [v0] + [swap(v0, 2 * e) for e in (1, 2, 3)]
    all_rows = width // HD * tokens
    qg0 = pl.pallas_call(
        pack_kernel,
        out_shape=shape((2 * all_rows, HD), bf16),
        in_specs=[smem, smem, vmem, vmem],
        out_specs=vmem,
        compiler_params=params,
        name="pack",
    )(comp_len[0], advantage[0], queries[0, 0], out_grad[0, 0])
    qg1 = swap(qg0, 1)
    qg2 = swap(qg0, 8)
    qg3 = swap(qg2, 1)
    qg = [qg0, qg1, qg2, qg3]
    counts = lax.all_to_all(
        jnp.broadcast_to(comp_len[0].astype(f32)[None], (prompts, 1)),
        "prompt",
        0,
        0,
        tiled=True,
    )
    count = jnp.sum(counts, axis=0)
    me = lax.axis_index("sample")
    info = jnp.stack([prompt_len[0]] + [me ^ (2 * e) for e in range(4)]).astype(jnp.int32)
    own_k, own_v = own_keys[0, 0], own_values[0, 0]
    stats0 = pl.pallas_call(
        functools.partial(stats_kernel, to_log2),
        out_shape=shape((56, HD), f32),
        in_specs=[smem, smem] + [vmem] * 14,
        out_specs=vmem,
        compiler_params=params,
        name="stats",
    )(info, count, *qg, *ks, *vs, own_k, own_v)
    stats = [stats0, swap(stats0, 1), swap(stats0, 8), swap(stats0, 9)]
    kv_rows = 2 * groups * block
    dq_rows = width // HD // 4 * HD
    outs = pl.pallas_call(
        functools.partial(grads_kernel, to_log2),
        out_shape=[
            shape((dq_rows, HD), f32),
            shape((dq_rows, HD), f32),
            shape((2 * dq_rows, HD), bf16),
            shape((kv_rows, HD), f32),
        ]
        + [shape((kv_rows + 16, HD), bf16)] * 3
        + [shape((2 * tokens, kv_width), f32), shape((8, HD), f32)],
        in_specs=[smem] + [vmem] * 18,
        out_specs=[vmem] * 9,
        compiler_params=params,
        name="grads",
    )(info, *qg, *ks, *vs, own_k, own_v, *stats)
    dq_own, dq_far, dq_sib, dkv_own = outs[:4]
    dq_core = swap(dq_sib, 1)
    dq_x = swap((dq_far + dq_core[dq_rows:].astype(f32)).astype(bf16), 8)
    received = [swap(outs[3 + e], 2 * e) for e in (1, 2, 3)]
    q_out, k_out, v_out, ok_out, ov_out = pl.pallas_call(
        functools.partial(finish_kernel, loss_top, softmax_scale),
        out_shape=[
            shape((tokens, width), bf16),
            shape((block, kv_width), bf16),
            shape((block, kv_width), bf16),
            shape((tokens, kv_width), bf16),
            shape((tokens, kv_width), bf16),
        ],
        in_specs=[vmem] * 9,
        out_specs=[vmem] * 5,
        compiler_params=params,
        name="finish",
    )(dq_own, dq_core, dq_x, dkv_own, *received, outs[7], outs[8])
    return (q_out[None, None], k_out[None], v_out[None], ok_out[None, None], ov_out[None, None])


def solution(mesh):
    in_specs = (
        P("prompt", "sample", None, None),
        P("prompt", "sample", None, None),
        P("prompt", "sample"),
        P("prompt", "sample"),
        P("prompt", "sample", None),
        P("prompt", "sample", None),
        P("prompt", "sample", None, None),
        P("prompt", "sample", None, None),
        P("prompt"),
    )
    out_specs = (
        P("prompt", "sample", None, None),
        P("prompt", "sample", None),
        P("prompt", "sample", None),
        P("prompt", "sample", None, None),
        P("prompt", "sample", None, None),
    )
    return jax.shard_map(
        per_device, mesh=mesh, in_specs=in_specs, out_specs=out_specs, check_vma=False
    )
```

```python
import functools
import math

import jax
import jax.numpy as jnp
from jax import lax
from jax.experimental import pallas as pl
from jax.experimental.pallas import tpu as pltpu
from jax.sharding import PartitionSpec as P

HD = 128
MASKED = -1e30
VMEM_LIMIT = 24 * 1024 * 1024
NT = (((1,), (1,)), ((), ()))
NN = (((1,), (0,)), ((), ()))


def dot(a, b, dims):
    return lax.dot_general(a, b, dims, preferred_element_type=jnp.float32)


def rows_of(refs, kind, g):
    tokens = refs[0].shape[0] // 2
    rows = slice(kind * tokens, (kind + 1) * tokens)
    return jnp.concatenate(
        [r[rows, h * HD : (h + 1) * HD] for r in refs for h in range(4 * g, 4 * g + 4)], axis=0
    )


def cols_of(refs, start, g):
    size = (refs[0].shape[0] - 16) // 2
    return jnp.concatenate(
        [r[start * size : (start + 1) * size, g * HD : (g + 1) * HD] for r in refs], axis=0
    )


def key_bias(info_ref, block):
    at = lax.broadcasted_iota(jnp.int32, (block, 1), 0)
    return jnp.concatenate(
        [
            jnp.where(at + info_ref[1 + k] * block < info_ref[0], 0.0, MASKED)
            for k in range(4)
        ],
        axis=0,
    )


def own_mask(tokens, rows):
    u = lax.broadcasted_iota(jnp.int32, (tokens, rows), 0)
    t = lax.broadcasted_iota(jnp.int32, (tokens, rows), 1) % tokens
    return u <= t


def stats_kernel(to_log2, info_ref, *refs):
    qg, kvs, own_ref, out_ref = refs[0:4], refs[4:8], refs[8], refs[9]
    block = (kvs[0].shape[0] - 16) // 2
    groups = kvs[0].shape[1] // HD
    tokens = own_ref.shape[0] // 2
    rows = qg[0].shape[1] // HD // groups * tokens
    bias = key_bias(info_ref, block)
    causal = own_mask(tokens, rows)
    out_ref[48:56, :] = sum(
        r[2 * block : 2 * block + 16, :HD].astype(jnp.float32)[:8] for r in kvs
    )
    for g in range(groups):
        q = rows_of(qg, 0, g)
        w = rows_of(qg, 1, g)
        score = dot(cols_of(kvs, 0, g), q, NT) * to_log2 + bias
        slope = dot(cols_of(kvs, 1, g), w, NT)
        own_cols = slice(g * HD, (g + 1) * HD)
        own_score = dot(own_ref[:tokens, own_cols], q[:rows], NT) * to_log2
        own_score = jnp.where(causal, own_score, MASKED)
        own_slope = dot(own_ref[tokens:, own_cols], w[:rows], NT)
        top = jnp.max(score, axis=0, keepdims=True)
        own_top = jnp.maximum(
            top[:, :rows], jnp.max(own_score, axis=0, keepdims=True)
        )
        top = jnp.concatenate([own_top, top[:, rows:]], axis=1)
        e = jnp.exp2(score - top)
        total = jnp.sum(e, axis=0, keepdims=True)
        mixed = jnp.sum(e * slope, axis=0, keepdims=True)
        own_e = jnp.exp2(own_score - own_top)
        own_total = jnp.sum(own_e, axis=0, keepdims=True)
        own_mixed = jnp.sum(own_e * own_slope, axis=0, keepdims=True)
        for s in range(4):
            lanes = slice(s * rows, (s + 1) * rows)
            at = s * 4 + g
            out_ref[at : at + 1, :] = top[:, lanes]
            extra = (own_total, own_mixed) if s == 0 else (0.0, 0.0)
            out_ref[16 + at : 17 + at, :] = total[:, lanes] + extra[0]
            out_ref[32 + at : 33 + at, :] = mixed[:, lanes] + extra[1]


def grads_kernel(to_log2, info_ref, *refs):
    qg, kvs, own_ref = refs[0:4], refs[4:8], refs[8]
    stats = refs[9:13]
    dq_own, dq_far, dq_sib, dkv_own = refs[13:17]
    dkv_out = refs[17:20]
    own_out, tot_out = refs[20:22]
    block = (kvs[0].shape[0] - 16) // 2
    groups = kvs[0].shape[1] // HD
    tokens = own_ref.shape[0] // 2
    rows = qg[0].shape[1] // HD // groups * tokens
    bias = key_bias(info_ref, block)
    causal = own_mask(tokens, rows)
    shifts, means = [], []
    for s in range(4):
        tops = [stats[e][(s ^ e) * 4 : (s ^ e) * 4 + 4, :] for e in range(4)]
        top = functools.reduce(jnp.maximum, tops)
        total, mixed = 0.0, 0.0
        for e in range(4):
            factor = jnp.exp2(tops[e] - top)
            at = (s ^ e) * 4
            total += stats[e][16 + at : 20 + at, :] * factor
            mixed += stats[e][32 + at : 36 + at, :] * factor
        shifts.append(top + jnp.log2(total))
        means.append(mixed / total)
    shift = jnp.concatenate(shifts, axis=1)
    mean = jnp.concatenate(means, axis=1)
    half = groups * block
    for i in range(tot_out.shape[0]):
        tot_out[i] = sum(stats[e][48:49, :] for e in range(4))
    for g in range(groups):
        q = rows_of(qg, 0, g)
        w = rows_of(qg, 1, g)
        k = cols_of(kvs, 0, g)
        sh, mn = shift[g : g + 1, :], mean[g : g + 1, :]
        score = dot(k, q, NT) * to_log2 + bias
        slope = dot(cols_of(kvs, 1, g), w, NT)
        p = jnp.exp2(score - sh)
        ds = (p * (slope - mn)).astype(jnp.bfloat16)
        dv = dot(p.astype(jnp.bfloat16), w, NN)
        dk = dot(ds, q, NN)
        dq = dot(k.T, ds, NN)
        own_cols = slice(g * HD, (g + 1) * HD)
        own_k = own_ref[:tokens, own_cols]
        own_score = dot(own_k, q[:rows], NT) * to_log2
        own_score = jnp.where(causal, own_score, MASKED)
        own_slope = dot(own_ref[tokens:, own_cols], w[:rows], NT)
        own_p = jnp.exp2(own_score - sh[:, :rows])
        own_ds = (own_p * (own_slope - mn[:, :rows])).astype(jnp.bfloat16)
        own_out[:tokens, own_cols] = dot(own_ds, q[:rows], NN)
        own_out[tokens:, own_cols] = dot(own_p.astype(jnp.bfloat16), w[:rows], NN)
        own_dq = dot(own_k.T, own_ds, NN)
        at = slice(g * HD, (g + 1) * HD)
        dq_own[at, :] = dq[:, :rows] + own_dq
        dq_far[at, :] = dq[:, 2 * rows : 3 * rows]
        dq_sib[at, :] = dq[:, rows : 2 * rows].astype(jnp.bfloat16)
        dq_sib[half_at(dq_sib, g), :] = dq[:, 3 * rows :].astype(jnp.bfloat16)
        here = slice(g * block, (g + 1) * block)
        there = slice(half + g * block, half + (g + 1) * block)
        dkv_own[here, :] = dk[:block]
        dkv_own[there, :] = dv[:block]
        for e in range(3):
            part = slice((e + 1) * block, (e + 2) * block)
            dkv_out[e][here, :] = dk[part].astype(jnp.bfloat16)
            dkv_out[e][there, :] = dv[part].astype(jnp.bfloat16)


def half_at(ref, g):
    half = ref.shape[0] // 2
    return slice(half + g * HD, half + (g + 1) * HD)


def finish_kernel(loss_top, softmax_scale, *refs):
    dq_own, dq_core, dq_x, dkv_own, r1, r2, r3, own_ref, tot_ref = refs[:9]
    q_out, k_out, v_out, ok_out, ov_out = refs[9:]
    block = k_out.shape[0]
    groups = k_out.shape[1] // HD
    tokens = ok_out.shape[0]
    per_group = q_out.shape[1] // HD // groups
    half = groups * block
    f32 = jnp.float32
    count = functools.reduce(jnp.add, [tot_ref[i] for i in range(tot_ref.shape[0])])
    scale = loss_top / count[:1, :]
    key_scale = scale * softmax_scale
    for g in range(groups):
        cols = slice(g * HD, (g + 1) * HD)
        dq = (
            dq_own[cols, :]
            + dq_core[cols, :].astype(f32)
            + dq_x[cols, :].astype(f32)
        ).T * key_scale
        for x in range(per_group):
            h = g * per_group + x
            q_out[:, h * HD : (h + 1) * HD] = dq[x * tokens : (x + 1) * tokens].astype(
                jnp.bfloat16
            )
        for out, start, by in ((k_out, 0, key_scale), (v_out, half, scale)):
            at = slice(start + g * block, start + (g + 1) * block)
            term = (dkv_own[at, :] + r1[at, :].astype(f32)) + (
                r2[at, :].astype(f32) + r3[at, :].astype(f32)
            )
            out[:, cols] = (term * by).astype(jnp.bfloat16)
        ok_out[:, cols] = (own_ref[:tokens, cols] * key_scale).astype(jnp.bfloat16)
        ov_out[:, cols] = (own_ref[tokens:, cols] * scale).astype(jnp.bfloat16)


def per_device(
    queries,
    out_grad,
    advantage,
    comp_len,
    prefix_keys,
    prefix_values,
    own_keys,
    own_values,
    prompt_len,
):
    samples = lax.axis_size("sample")
    prompts = lax.axis_size("prompt")
    tokens, width = queries.shape[2], queries.shape[3]
    block, kv_width = prefix_keys.shape[1], prefix_keys.shape[2]
    groups = kv_width // HD
    softmax_scale = 1.0 / math.sqrt(HD)
    to_log2 = softmax_scale * math.log2(math.e)
    loss_top = prompts * samples * tokens * math.sqrt(block * samples) / 4.0
    bf16, f32 = jnp.bfloat16, jnp.float32
    vmem = pl.BlockSpec(memory_space=pltpu.VMEM)
    smem = pl.BlockSpec(memory_space=pltpu.SMEM)
    params = pltpu.CompilerParams(vmem_limit_bytes=VMEM_LIMIT)
    shape = jax.ShapeDtypeStruct

    def swap(array, mask):
        return lax.ppermute(array, "sample", [(i, i ^ mask) for i in range(samples)])

    at = lax.broadcasted_iota(jnp.int32, (tokens, width), 0)
    weight = jnp.where(at < comp_len[0, 0], advantage[0, 0], 0.0)
    weighted = (out_grad[0, 0].astype(f32) * weight).astype(bf16)
    mark = jnp.broadcast_to(comp_len.astype(bf16), (16, kv_width))
    kv0 = jnp.concatenate([prefix_keys[0], prefix_values[0], mark], axis=0)
    qg0 = jnp.concatenate([queries[0, 0], weighted], axis=0)
    own = jnp.concatenate([own_keys[0, 0], own_values[0, 0]], axis=0)
    qg2 = swap(qg0, 8)
    kv = [kv0] + [swap(kv0, 2 * e) for e in (1, 2, 3)]
    qg1 = swap(qg0, 1)
    qg3 = swap(qg2, 1)
    qg = [qg0, qg1, qg2, qg3]
    me = lax.axis_index("sample")
    info = jnp.stack([prompt_len[0]] + [me ^ (2 * e) for e in range(4)]).astype(jnp.int32)
    stats0 = pl.pallas_call(
        functools.partial(stats_kernel, to_log2),
        out_shape=shape((56, HD), f32),
        in_specs=[smem] + [vmem] * 9,
        out_specs=vmem,
        compiler_params=params,
        name="stats",
    )(info, *qg, *kv, own)
    stats = [stats0, swap(stats0, 1), swap(stats0, 8), swap(stats0, 9)]
    kv_rows = 2 * groups * block
    dq_rows = width // HD // 4 * HD
    outs = pl.pallas_call(
        functools.partial(grads_kernel, to_log2),
        out_shape=[
            shape((dq_rows, HD), f32),
            shape((dq_rows, HD), f32),
            shape((2 * dq_rows, HD), bf16),
            shape((kv_rows, HD), f32),
        ]
        + [shape((kv_rows, HD), bf16)] * 3
        + [shape((2 * tokens, kv_width), f32), shape((prompts, 1, HD), f32)],
        in_specs=[smem] + [vmem] * 13,
        out_specs=[vmem] * 9,
        compiler_params=params,
        name="grads",
    )(info, *qg, *kv, own, *stats)
    dq_own, dq_far, dq_sib, dkv_own = outs[:4]
    dq_core = swap(dq_sib, 1)
    dq_x = swap((dq_far + dq_core[dq_rows:].astype(f32)).astype(bf16), 8)
    total = lax.all_to_all(outs[8], "prompt", 0, 0, tiled=True)
    received = [swap(outs[3 + e], 2 * e) for e in (1, 2, 3)]
    q_out, k_out, v_out, ok_out, ov_out = pl.pallas_call(
        functools.partial(finish_kernel, loss_top, softmax_scale),
        out_shape=[
            shape((tokens, width), bf16),
            shape((block, kv_width), bf16),
            shape((block, kv_width), bf16),
            shape((tokens, kv_width), bf16),
            shape((tokens, kv_width), bf16),
        ],
        in_specs=[vmem] * 9,
        out_specs=[vmem] * 5,
        compiler_params=params,
        name="finish",
    )(dq_own, dq_core, dq_x, dkv_own, *received, outs[7], total)
    return (q_out[None, None], k_out[None], v_out[None], ok_out[None, None], ov_out[None, None])


def solution(mesh):
    in_specs = (
        P("prompt", "sample", None, None),
        P("prompt", "sample", None, None),
        P("prompt", "sample"),
        P("prompt", "sample"),
        P("prompt", "sample", None),
        P("prompt", "sample", None),
        P("prompt", "sample", None, None),
        P("prompt", "sample", None, None),
        P("prompt"),
    )
    out_specs = (
        P("prompt", "sample", None, None),
        P("prompt", "sample", None),
        P("prompt", "sample", None),
        P("prompt", "sample", None, None),
        P("prompt", "sample", None, None),
    )
    return jax.shard_map(
        per_device, mesh=mesh, in_specs=in_specs, out_specs=out_specs, check_vma=False
    )
```

```python
import functools
import math

import jax
import jax.numpy as jnp
from jax import lax
from jax.experimental import pallas as pl
from jax.experimental.pallas import tpu as pltpu
from jax.sharding import PartitionSpec as P

HD = 128
MASKED = -1e30
VMEM_LIMIT = 24 * 1024 * 1024
NT = (((1,), (1,)), ((), ()))
NN = (((1,), (0,)), ((), ()))


def dot(a, b, dims):
    return lax.dot_general(a, b, dims, preferred_element_type=jnp.float32)


def rows_of(refs, kind, g):
    tokens = refs[0].shape[0] // 2
    rows = slice(kind * tokens, (kind + 1) * tokens)
    return jnp.concatenate(
        [r[rows, h * HD : (h + 1) * HD] for r in refs for h in range(4 * g, 4 * g + 4)], axis=0
    )


def cols_of(refs, start, g):
    size = (refs[0].shape[0] - 16) // 2
    return jnp.concatenate(
        [r[start * size : (start + 1) * size, g * HD : (g + 1) * HD] for r in refs], axis=0
    )


def own_bias(tokens, rows):
    u = lax.broadcasted_iota(jnp.int32, (tokens, 4 * rows), 0)
    lane = lax.broadcasted_iota(jnp.int32, (tokens, 4 * rows), 1)
    return jnp.where((lane < rows) & (u <= lane % tokens), 0.0, MASKED)


def block_bias(info_ref, k, block):
    at = lax.broadcasted_iota(jnp.int32, (block, 1), 0)
    return jnp.where(at + info_ref[1 + k] * block < info_ref[0], 0.0, MASKED)


def with_own(blocks, own_ref, part, g):
    tokens = own_ref.shape[0] // 2
    own = own_ref[part * tokens : (part + 1) * tokens, g * HD : (g + 1) * HD]
    return jnp.concatenate([cols_of(blocks, part, g), own], axis=0)


def partial_stats(score, slope):
    top = jnp.max(score, axis=0, keepdims=True)
    e = jnp.exp2(score - top)
    total = jnp.sum(e, axis=0, keepdims=True)
    return top, total, jnp.sum(e * slope, axis=0, keepdims=True)


def add_bias(score, bias, own):
    at = bias.shape[0]
    return jnp.concatenate([score[:at] + bias, score[at:] + own], axis=0)


def join(one, two):
    top = jnp.maximum(one[0], two[0])
    f, h = jnp.exp2(one[0] - top), jnp.exp2(two[0] - top)
    return top, one[1] * f + two[1] * h, one[2] * f + two[2] * h


def first_stats_kernel(to_log2, where, info_ref, *refs):
    qg, kvs, own_ref, out_ref = refs[0:4], refs[4:-2], refs[-2], refs[-1]
    block = (kvs[0].shape[0] - 16) // 2
    groups = kvs[0].shape[1] // HD
    tokens = own_ref.shape[0] // 2
    rows = qg[0].shape[1] // HD // groups * tokens
    bias = jnp.concatenate([block_bias(info_ref, k, block) for k in where], axis=0)
    own = own_bias(tokens, rows)
    out_ref[...] = jnp.zeros_like(out_ref)
    for g in range(groups):
        q, w = rows_of(qg, 0, g), rows_of(qg, 1, g)
        score = dot(with_own(kvs, own_ref, 0, g), q, NT) * to_log2
        slope = dot(with_own(kvs, own_ref, 1, g), w, NT)
        for i, value in enumerate(partial_stats(add_bias(score, bias, own), slope)):
            out_ref[i * groups + g : i * groups + g + 1, :] = value


def last_stats_kernel(to_log2, where, info_ref, *refs):
    qg, kvs, first_ref, out_ref = refs[0:4], refs[4:8], refs[8], refs[9]
    block = (kvs[0].shape[0] - 16) // 2
    groups = kvs[0].shape[1] // HD
    rows = qg[0].shape[1] // HD // groups * (qg[0].shape[0] // 2)
    bias = jnp.concatenate([block_bias(info_ref, k, block) for k in where], axis=0)
    out_ref[48:56, :] = sum(
        r[2 * block : 2 * block + 16, :HD].astype(jnp.float32)[:8] for r in kvs
    )
    for g in range(groups):
        q, w = rows_of(qg, 0, g), rows_of(qg, 1, g)
        blocks = [kvs[k] for k in where]
        score = dot(cols_of(blocks, 0, g), q, NT) * to_log2 + bias
        got = partial_stats(score, dot(cols_of(blocks, 1, g), w, NT))
        before = [first_ref[i * groups + g : i * groups + g + 1, :] for i in range(3)]
        got = join(before, got)
        for s in range(4):
            for i in range(3):
                at = 16 * i + 4 * s + g
                out_ref[at : at + 1, :] = got[i][:, s * rows : (s + 1) * rows]


def grads_kernel(to_log2, info_ref, *refs):
    qg, kvs, own_ref = refs[0:4], refs[4:8], refs[8]
    stats = refs[9:13]
    dq_own, dq_far, dq_sib, dkv_own = refs[13:17]
    dkv_out = refs[17:20]
    own_out, tot_out = refs[20:22]
    block = (kvs[0].shape[0] - 16) // 2
    groups = kvs[0].shape[1] // HD
    tokens = own_ref.shape[0] // 2
    rows = qg[0].shape[1] // HD // groups * tokens
    bias = jnp.concatenate([block_bias(info_ref, k, block) for k in range(4)], axis=0)
    own_rows = own_bias(tokens, rows)
    shifts, means = [], []
    for s in range(4):
        tops = [stats[e][(s ^ e) * 4 : (s ^ e) * 4 + 4, :] for e in range(4)]
        top = functools.reduce(jnp.maximum, tops)
        total, mixed = 0.0, 0.0
        for e in range(4):
            factor = jnp.exp2(tops[e] - top)
            at = (s ^ e) * 4
            total += stats[e][16 + at : 20 + at, :] * factor
            mixed += stats[e][32 + at : 36 + at, :] * factor
        shifts.append(top + jnp.log2(total))
        means.append(mixed / total)
    shift = jnp.concatenate(shifts, axis=1)
    mean = jnp.concatenate(means, axis=1)
    half = groups * block
    for i in range(tot_out.shape[0]):
        tot_out[i] = sum(stats[e][48:49, :] for e in range(4))
    for g in range(groups):
        q = rows_of(qg, 0, g)
        w = rows_of(qg, 1, g)
        k = with_own(kvs, own_ref, 0, g)
        sh, mn = shift[g : g + 1, :], mean[g : g + 1, :]
        score = add_bias(dot(k, q, NT) * to_log2, bias, own_rows)
        slope = dot(with_own(kvs, own_ref, 1, g), w, NT)
        p = jnp.exp2(score - sh)
        ds = (p * (slope - mn)).astype(jnp.bfloat16)
        dv = dot(p.astype(jnp.bfloat16), w, NN)
        dk = dot(ds, q, NN)
        dq = dot(k.T, ds, NN)
        own_cols = slice(g * HD, (g + 1) * HD)
        own_out[:tokens, own_cols] = dk[4 * block :]
        own_out[tokens:, own_cols] = dv[4 * block :]
        at = slice(g * HD, (g + 1) * HD)
        dq_own[at, :] = dq[:, :rows]
        dq_far[at, :] = dq[:, 2 * rows : 3 * rows]
        dq_sib[at, :] = dq[:, rows : 2 * rows].astype(jnp.bfloat16)
        dq_sib[half_at(dq_sib, g), :] = dq[:, 3 * rows :].astype(jnp.bfloat16)
        here = slice(g * block, (g + 1) * block)
        there = slice(half + g * block, half + (g + 1) * block)
        dkv_own[here, :] = dk[:block]
        dkv_own[there, :] = dv[:block]
        for e in range(3):
            part = slice((e + 1) * block, (e + 2) * block)
            dkv_out[e][here, :] = dk[part].astype(jnp.bfloat16)
            dkv_out[e][there, :] = dv[part].astype(jnp.bfloat16)


def half_at(ref, g):
    half = ref.shape[0] // 2
    return slice(half + g * HD, half + (g + 1) * HD)


def finish_kernel(loss_top, softmax_scale, *refs):
    dq_own, dq_core, dq_x, dkv_own, r1, r2, r3, own_ref, tot_ref = refs[:9]
    q_out, k_out, v_out, ok_out, ov_out = refs[9:]
    block = k_out.shape[0]
    groups = k_out.shape[1] // HD
    tokens = ok_out.shape[0]
    per_group = q_out.shape[1] // HD // groups
    half = groups * block
    f32 = jnp.float32
    count = functools.reduce(jnp.add, [tot_ref[i] for i in range(tot_ref.shape[0])])
    scale = loss_top / count[:1, :]
    key_scale = scale * softmax_scale
    for g in range(groups):
        cols = slice(g * HD, (g + 1) * HD)
        dq = (
            dq_own[cols, :]
            + dq_core[cols, :].astype(f32)
            + dq_x[cols, :].astype(f32)
        ).T * key_scale
        for x in range(per_group):
            h = g * per_group + x
            q_out[:, h * HD : (h + 1) * HD] = dq[x * tokens : (x + 1) * tokens].astype(
                jnp.bfloat16
            )
        for out, start, by in ((k_out, 0, key_scale), (v_out, half, scale)):
            at = slice(start + g * block, start + (g + 1) * block)
            term = (dkv_own[at, :] + r1[at, :].astype(f32)) + (
                r2[at, :].astype(f32) + r3[at, :].astype(f32)
            )
            out[:, cols] = (term * by).astype(jnp.bfloat16)
        ok_out[:, cols] = (own_ref[:tokens, cols] * key_scale).astype(jnp.bfloat16)
        ov_out[:, cols] = (own_ref[tokens:, cols] * scale).astype(jnp.bfloat16)


def per_device(
    queries,
    out_grad,
    advantage,
    comp_len,
    prefix_keys,
    prefix_values,
    own_keys,
    own_values,
    prompt_len,
):
    samples = lax.axis_size("sample")
    prompts = lax.axis_size("prompt")
    tokens, width = queries.shape[2], queries.shape[3]
    block, kv_width = prefix_keys.shape[1], prefix_keys.shape[2]
    groups = kv_width // HD
    softmax_scale = 1.0 / math.sqrt(HD)
    to_log2 = softmax_scale * math.log2(math.e)
    loss_top = prompts * samples * tokens * math.sqrt(block * samples) / 4.0
    bf16, f32 = jnp.bfloat16, jnp.float32
    vmem = pl.BlockSpec(memory_space=pltpu.VMEM)
    smem = pl.BlockSpec(memory_space=pltpu.SMEM)
    params = pltpu.CompilerParams(vmem_limit_bytes=VMEM_LIMIT)
    shape = jax.ShapeDtypeStruct

    def swap(array, mask):
        return lax.ppermute(array, "sample", [(i, i ^ mask) for i in range(samples)])

    at = lax.broadcasted_iota(jnp.int32, (tokens, width), 0)
    weight = jnp.where(at < comp_len[0, 0], advantage[0, 0], 0.0)
    weighted = (out_grad[0, 0].astype(f32) * weight).astype(bf16)
    mark = jnp.broadcast_to(comp_len.astype(bf16), (16, kv_width))
    kv0 = jnp.concatenate([prefix_keys[0], prefix_values[0], mark], axis=0)
    qg0 = jnp.concatenate([queries[0, 0], weighted], axis=0)
    own = jnp.concatenate([own_keys[0, 0], own_values[0, 0]], axis=0)
    qg2 = swap(qg0, 8)
    kv = [kv0] + [swap(kv0, 2 * e) for e in (1, 2, 3)]
    qg1 = swap(qg0, 1)
    qg3 = swap(qg2, 1)
    qg = [qg0, qg1, qg2, qg3]
    me = lax.axis_index("sample")
    info = jnp.stack([prompt_len[0]] + [me ^ (2 * e) for e in range(4)]).astype(jnp.int32)
    early, late = (0, 1, 3), (2,)
    first = pl.pallas_call(
        functools.partial(first_stats_kernel, to_log2, early),
        out_shape=shape((16, width * 4 * tokens // HD // groups), f32),
        in_specs=[smem] + [vmem] * (5 + len(early)),
        out_specs=vmem,
        compiler_params=params,
        name="stats_first",
    )(info, *qg, *[kv[k] for k in early], own)
    stats0 = pl.pallas_call(
        functools.partial(last_stats_kernel, to_log2, late),
        out_shape=shape((56, HD), f32),
        in_specs=[smem] + [vmem] * 9,
        out_specs=vmem,
        compiler_params=params,
        name="stats",
    )(info, *qg, *kv, first)
    stats = [stats0, swap(stats0, 1), swap(stats0, 8), swap(stats0, 9)]
    kv_rows = 2 * groups * block
    dq_rows = width // HD // 4 * HD
    outs = pl.pallas_call(
        functools.partial(grads_kernel, to_log2),
        out_shape=[
            shape((dq_rows, HD), f32),
            shape((dq_rows, HD), f32),
            shape((2 * dq_rows, HD), bf16),
            shape((kv_rows, HD), f32),
        ]
        + [shape((kv_rows, HD), bf16)] * 3
        + [shape((2 * tokens, kv_width), f32), shape((prompts, 1, HD), f32)],
        in_specs=[smem] + [vmem] * 13,
        out_specs=[vmem] * 9,
        compiler_params=params,
        name="grads",
    )(info, *qg, *kv, own, *stats)
    dq_own, dq_far, dq_sib, dkv_own = outs[:4]
    dq_core = swap(dq_sib, 1)
    dq_x = swap((dq_far + dq_core[dq_rows:].astype(f32)).astype(bf16), 8)
    total = lax.all_to_all(outs[8], "prompt", 0, 0, tiled=True)
    received = [swap(outs[3 + e], 2 * e) for e in (1, 2, 3)]
    q_out, k_out, v_out, ok_out, ov_out = pl.pallas_call(
        functools.partial(finish_kernel, loss_top, softmax_scale),
        out_shape=[
            shape((tokens, width), bf16),
            shape((block, kv_width), bf16),
            shape((block, kv_width), bf16),
            shape((tokens, kv_width), bf16),
            shape((tokens, kv_width), bf16),
        ],
        in_specs=[vmem] * 9,
        out_specs=[vmem] * 5,
        compiler_params=params,
        name="finish",
    )(dq_own, dq_core, dq_x, dkv_own, *received, outs[7], total)
    return (q_out[None, None], k_out[None], v_out[None], ok_out[None, None], ov_out[None, None])


def solution(mesh):
    in_specs = (
        P("prompt", "sample", None, None),
        P("prompt", "sample", None, None),
        P("prompt", "sample"),
        P("prompt", "sample"),
        P("prompt", "sample", None),
        P("prompt", "sample", None),
        P("prompt", "sample", None, None),
        P("prompt", "sample", None, None),
        P("prompt"),
    )
    out_specs = (
        P("prompt", "sample", None, None),
        P("prompt", "sample", None),
        P("prompt", "sample", None),
        P("prompt", "sample", None, None),
        P("prompt", "sample", None, None),
    )
    return jax.shard_map(
        per_device, mesh=mesh, in_specs=in_specs, out_specs=out_specs, check_vma=False
    )
```

```python
import functools
import math

import jax
import jax.numpy as jnp
from jax import lax
from jax.experimental import pallas as pl
from jax.experimental.pallas import tpu as pltpu
from jax.sharding import PartitionSpec as P

HD = 128
MASKED = -1e30
VMEM_LIMIT = 24 * 1024 * 1024
NT = (((1,), (1,)), ((), ()))
NN = (((1,), (0,)), ((), ()))


def dot(a, b, dims):
    return lax.dot_general(a, b, dims, preferred_element_type=jnp.float32)


def rows_of(refs, kind, g):
    tokens = refs[0].shape[0] // 2
    rows = slice(kind * tokens, (kind + 1) * tokens)
    return jnp.concatenate(
        [r[rows, h * HD : (h + 1) * HD] for r in refs for h in range(4 * g, 4 * g + 4)], axis=0
    )


def cols_of(refs, start, g):
    size = (refs[0].shape[0] - 16) // 2
    return jnp.concatenate(
        [r[start * size : (start + 1) * size, g * HD : (g + 1) * HD] for r in refs], axis=0
    )


def own_bias(tokens, rows):
    u = lax.broadcasted_iota(jnp.int32, (tokens, 4 * rows), 0)
    lane = lax.broadcasted_iota(jnp.int32, (tokens, 4 * rows), 1)
    return jnp.where((lane < rows) & (u <= lane % tokens), 0.0, MASKED)


def block_bias(info_ref, k, block):
    at = lax.broadcasted_iota(jnp.int32, (block, 1), 0)
    return jnp.where(at + info_ref[1 + k] * block < info_ref[0], 0.0, MASKED)


def with_own(blocks, own_ref, part, g):
    tokens = own_ref.shape[0] // 2
    own = own_ref[part * tokens : (part + 1) * tokens, g * HD : (g + 1) * HD]
    return jnp.concatenate([cols_of(blocks, part, g), own], axis=0)


def partial_stats(score, slope):
    top = jnp.max(score, axis=0, keepdims=True)
    e = jnp.exp2(score - top)
    total = jnp.sum(e, axis=0, keepdims=True)
    return top, total, jnp.sum(e * slope, axis=0, keepdims=True)


def add_bias(score, bias, own):
    at = bias.shape[0]
    return jnp.concatenate([score[:at] + bias, score[at:] + own], axis=0)


def join(one, two):
    top = jnp.maximum(one[0], two[0])
    f, h = jnp.exp2(one[0] - top), jnp.exp2(two[0] - top)
    return top, one[1] * f + two[1] * h, one[2] * f + two[2] * h


def pass_kernel(*refs):
    pass


def first_stats_kernel(to_log2, where, info_ref, *refs):
    qg, kvs, own_ref, out_ref = refs[0:4], refs[4:-2], refs[-2], refs[-1]
    block = (kvs[0].shape[0] - 16) // 2
    groups = kvs[0].shape[1] // HD
    tokens = own_ref.shape[0] // 2
    rows = qg[0].shape[1] // HD // groups * tokens
    bias = jnp.concatenate([block_bias(info_ref, k, block) for k in where], axis=0)
    own = own_bias(tokens, rows)
    out_ref[...] = jnp.zeros_like(out_ref)
    for g in range(groups):
        q, w = rows_of(qg, 0, g), rows_of(qg, 1, g)
        score = dot(with_own(kvs, own_ref, 0, g), q, NT) * to_log2
        slope = dot(with_own(kvs, own_ref, 1, g), w, NT)
        for i, value in enumerate(partial_stats(add_bias(score, bias, own), slope)):
            out_ref[i * groups + g : i * groups + g + 1, :] = value


def last_stats_kernel(to_log2, where, info_ref, *refs):
    qg, kvs, first_ref, out_ref = refs[0:4], refs[4:8], refs[8], refs[9]
    block = (kvs[0].shape[0] - 16) // 2
    groups = kvs[0].shape[1] // HD
    rows = qg[0].shape[1] // HD // groups * (qg[0].shape[0] // 2)
    bias = jnp.concatenate([block_bias(info_ref, k, block) for k in where], axis=0)
    out_ref[48:56, :] = sum(
        r[2 * block : 2 * block + 16, :HD].astype(jnp.float32)[:8] for r in kvs
    )
    for g in range(groups):
        q, w = rows_of(qg, 0, g), rows_of(qg, 1, g)
        blocks = [kvs[k] for k in where]
        score = dot(cols_of(blocks, 0, g), q, NT) * to_log2 + bias
        got = partial_stats(score, dot(cols_of(blocks, 1, g), w, NT))
        before = [first_ref[i * groups + g : i * groups + g + 1, :] for i in range(3)]
        got = join(before, got)
        for s in range(4):
            for i in range(3):
                at = 16 * i + 4 * s + g
                out_ref[at : at + 1, :] = got[i][:, s * rows : (s + 1) * rows]


def grads_kernel(to_log2, info_ref, *refs):
    qg, kvs, own_ref = refs[0:4], refs[4:8], refs[8]
    stats = refs[9:13]
    dq_own, dq_far, dq_sib, dkv_own = refs[13:17]
    dkv_out = refs[17:20]
    own_out, tot_out = refs[20:22]
    block = (kvs[0].shape[0] - 16) // 2
    groups = kvs[0].shape[1] // HD
    tokens = own_ref.shape[0] // 2
    rows = qg[0].shape[1] // HD // groups * tokens
    bias = jnp.concatenate([block_bias(info_ref, k, block) for k in range(4)], axis=0)
    own_rows = own_bias(tokens, rows)
    shifts, means = [], []
    for s in range(4):
        tops = [stats[e][(s ^ e) * 4 : (s ^ e) * 4 + 4, :] for e in range(4)]
        top = functools.reduce(jnp.maximum, tops)
        total, mixed = 0.0, 0.0
        for e in range(4):
            factor = jnp.exp2(tops[e] - top)
            at = (s ^ e) * 4
            total += stats[e][16 + at : 20 + at, :] * factor
            mixed += stats[e][32 + at : 36 + at, :] * factor
        shifts.append(top + jnp.log2(total))
        means.append(mixed / total)
    shift = jnp.concatenate(shifts, axis=1)
    mean = jnp.concatenate(means, axis=1)
    half = groups * block
    for i in range(tot_out.shape[0]):
        tot_out[i] = sum(stats[e][48:49, :] for e in range(4))
    for g in range(groups):
        q = rows_of(qg, 0, g)
        w = rows_of(qg, 1, g)
        k = with_own(kvs, own_ref, 0, g)
        sh, mn = shift[g : g + 1, :], mean[g : g + 1, :]
        score = add_bias(dot(k, q, NT) * to_log2, bias, own_rows)
        slope = dot(with_own(kvs, own_ref, 1, g), w, NT)
        p = jnp.exp2(score - sh)
        ds = (p * (slope - mn)).astype(jnp.bfloat16)
        dv = dot(p.astype(jnp.bfloat16), w, NN)
        dk = dot(ds, q, NN)
        dq = dot(k.T, ds, NN)
        own_cols = slice(g * HD, (g + 1) * HD)
        own_out[:tokens, own_cols] = dk[4 * block :]
        own_out[tokens:, own_cols] = dv[4 * block :]
        at = slice(g * HD, (g + 1) * HD)
        dq_own[at, :] = dq[:, :rows]
        dq_far[at, :] = dq[:, 2 * rows : 3 * rows]
        dq_sib[at, :] = dq[:, rows : 2 * rows].astype(jnp.bfloat16)
        dq_sib[half_at(dq_sib, g), :] = dq[:, 3 * rows :].astype(jnp.bfloat16)
        here = slice(g * block, (g + 1) * block)
        there = slice(half + g * block, half + (g + 1) * block)
        dkv_own[here, :] = dk[:block]
        dkv_own[there, :] = dv[:block]
        for e in range(3):
            part = slice((e + 1) * block, (e + 2) * block)
            dkv_out[e][here, :] = dk[part].astype(jnp.bfloat16)
            dkv_out[e][there, :] = dv[part].astype(jnp.bfloat16)


def half_at(ref, g):
    half = ref.shape[0] // 2
    return slice(half + g * HD, half + (g + 1) * HD)


def finish_kernel(loss_top, softmax_scale, *refs):
    dq_own, dq_core, dq_x, dkv_own, r1, r2, r3, own_ref, tot_ref = refs[:9]
    q_out, k_out, v_out, ok_out, ov_out = refs[9:]
    block = k_out.shape[0]
    groups = k_out.shape[1] // HD
    tokens = ok_out.shape[0]
    per_group = q_out.shape[1] // HD // groups
    half = groups * block
    f32 = jnp.float32
    count = functools.reduce(jnp.add, [tot_ref[i] for i in range(tot_ref.shape[0])])
    scale = loss_top / count[:1, :]
    key_scale = scale * softmax_scale
    for g in range(groups):
        cols = slice(g * HD, (g + 1) * HD)
        dq = (
            dq_own[cols, :]
            + dq_core[cols, :].astype(f32)
            + dq_x[cols, :].astype(f32)
        ).T * key_scale
        for x in range(per_group):
            h = g * per_group + x
            q_out[:, h * HD : (h + 1) * HD] = dq[x * tokens : (x + 1) * tokens].astype(
                jnp.bfloat16
            )
        for out, start, by in ((k_out, 0, key_scale), (v_out, half, scale)):
            at = slice(start + g * block, start + (g + 1) * block)
            term = (dkv_own[at, :] + r1[at, :].astype(f32)) + (
                r2[at, :].astype(f32) + r3[at, :].astype(f32)
            )
            out[:, cols] = (term * by).astype(jnp.bfloat16)
        ok_out[:, cols] = (own_ref[:tokens, cols] * key_scale).astype(jnp.bfloat16)
        ov_out[:, cols] = (own_ref[tokens:, cols] * scale).astype(jnp.bfloat16)


def per_device(
    queries,
    out_grad,
    advantage,
    comp_len,
    prefix_keys,
    prefix_values,
    own_keys,
    own_values,
    prompt_len,
):
    samples = lax.axis_size("sample")
    prompts = lax.axis_size("prompt")
    tokens, width = queries.shape[2], queries.shape[3]
    block, kv_width = prefix_keys.shape[1], prefix_keys.shape[2]
    groups = kv_width // HD
    softmax_scale = 1.0 / math.sqrt(HD)
    to_log2 = softmax_scale * math.log2(math.e)
    loss_top = prompts * samples * tokens * math.sqrt(block * samples) / 4.0
    bf16, f32 = jnp.bfloat16, jnp.float32
    vmem = pl.BlockSpec(memory_space=pltpu.VMEM)
    smem = pl.BlockSpec(memory_space=pltpu.SMEM)
    params = pltpu.CompilerParams(vmem_limit_bytes=VMEM_LIMIT)
    shape = jax.ShapeDtypeStruct

    def swap(array, mask):
        return lax.ppermute(array, "sample", [(i, i ^ mask) for i in range(samples)])

    at = lax.broadcasted_iota(jnp.int32, (tokens, width), 0)
    weight = jnp.where(at < comp_len[0, 0], advantage[0, 0], 0.0)
    weighted = (out_grad[0, 0].astype(f32) * weight).astype(bf16)
    mark = jnp.broadcast_to(comp_len.astype(bf16), (16, kv_width))
    kv0 = jnp.concatenate([prefix_keys[0], prefix_values[0], mark], axis=0)
    qg0 = jnp.concatenate([queries[0, 0], weighted], axis=0)
    own = jnp.concatenate([own_keys[0, 0], own_values[0, 0]], axis=0)
    qg2 = swap(qg0, 8)
    kv = [kv0] + [swap(kv0, 2 * e) for e in (1, 2, 3)]
    kv[2], = pl.pallas_call(
        pass_kernel,
        out_shape=[shape(kv0.shape, bf16)] * 1,
        in_specs=[pl.BlockSpec(memory_space=pl.ANY)] * 1,
        out_specs=[pl.BlockSpec(memory_space=pl.ANY)] * 1,
        input_output_aliases={0: 0},
        cost_estimate=pl.CostEstimate(flops=20000000000, bytes_accessed=0, transcendentals=0),
        compiler_params=params,
        name="rows_here",
    )(kv[2])
    qg1 = swap(qg0, 1)
    qg3 = swap(qg2, 1)
    qg = [qg0, qg1, qg2, qg3]
    me = lax.axis_index("sample")
    info = jnp.stack([prompt_len[0]] + [me ^ (2 * e) for e in range(4)]).astype(jnp.int32)
    early, late = (0, 2), (1, 3)
    first = pl.pallas_call(
        functools.partial(first_stats_kernel, to_log2, early),
        out_shape=shape((16, width * 4 * tokens // HD // groups), f32),
        in_specs=[smem] + [vmem] * (5 + len(early)),
        out_specs=vmem,
        compiler_params=params,
        name="stats_first",
    )(info, *qg, *[kv[k] for k in early], own)
    stats0 = pl.pallas_call(
        functools.partial(last_stats_kernel, to_log2, late),
        out_shape=shape((56, HD), f32),
        in_specs=[smem] + [vmem] * 9,
        out_specs=vmem,
        compiler_params=params,
        name="stats",
    )(info, *qg, *kv, first)
    stats = [stats0, swap(stats0, 1), swap(stats0, 8), swap(stats0, 9)]
    kv_rows = 2 * groups * block
    dq_rows = width // HD // 4 * HD
    outs = pl.pallas_call(
        functools.partial(grads_kernel, to_log2),
        out_shape=[
            shape((dq_rows, HD), f32),
            shape((dq_rows, HD), f32),
            shape((2 * dq_rows, HD), bf16),
            shape((kv_rows, HD), f32),
        ]
        + [shape((kv_rows, HD), bf16)] * 3
        + [shape((2 * tokens, kv_width), f32), shape((prompts, 1, HD), f32)],
        in_specs=[smem] + [vmem] * 13,
        out_specs=[vmem] * 9,
        compiler_params=params,
        name="grads",
    )(info, *qg, *kv, own, *stats)
    dq_own, dq_far, dq_sib, dkv_own = outs[:4]
    dq_core = swap(dq_sib, 1)
    dq_x = swap((dq_far + dq_core[dq_rows:].astype(f32)).astype(bf16), 8)
    total = lax.all_to_all(outs[8], "prompt", 0, 0, tiled=True)
    received = [swap(outs[3 + e], 2 * e) for e in (1, 2, 3)]
    q_out, k_out, v_out, ok_out, ov_out = pl.pallas_call(
        functools.partial(finish_kernel, loss_top, softmax_scale),
        out_shape=[
            shape((tokens, width), bf16),
            shape((block, kv_width), bf16),
            shape((block, kv_width), bf16),
            shape((tokens, kv_width), bf16),
            shape((tokens, kv_width), bf16),
        ],
        in_specs=[vmem] * 9,
        out_specs=[vmem] * 5,
        compiler_params=params,
        name="finish",
    )(dq_own, dq_core, dq_x, dkv_own, *received, outs[7], total)
    return (q_out[None, None], k_out[None], v_out[None], ok_out[None, None], ov_out[None, None])


def solution(mesh):
    in_specs = (
        P("prompt", "sample", None, None),
        P("prompt", "sample", None, None),
        P("prompt", "sample"),
        P("prompt", "sample"),
        P("prompt", "sample", None),
        P("prompt", "sample", None),
        P("prompt", "sample", None, None),
        P("prompt", "sample", None, None),
        P("prompt"),
    )
    out_specs = (
        P("prompt", "sample", None, None),
        P("prompt", "sample", None),
        P("prompt", "sample", None),
        P("prompt", "sample", None, None),
        P("prompt", "sample", None, None),
    )
    return jax.shard_map(
        per_device, mesh=mesh, in_specs=in_specs, out_specs=out_specs, check_vma=False
    )
```

```python
import functools
import math

import jax
import jax.numpy as jnp
from jax import lax
from jax.experimental import pallas as pl
from jax.experimental.pallas import tpu as pltpu
from jax.sharding import PartitionSpec as P

HD = 128
MASKED = -1e30
VMEM_LIMIT = 24 * 1024 * 1024
NT = (((1,), (1,)), ((), ()))
NN = (((1,), (0,)), ((), ()))


def dot(a, b, dims):
    return lax.dot_general(a, b, dims, preferred_element_type=jnp.float32)


def rows_of(refs, kind, g):
    tokens = refs[0].shape[0] // 2
    rows = slice(kind * tokens, (kind + 1) * tokens)
    return jnp.concatenate(
        [r[rows, h * HD : (h + 1) * HD] for r in refs for h in range(4 * g, 4 * g + 4)], axis=0
    )


def cols_of(refs, start, g):
    size = (refs[0].shape[0] - 16) // 2
    return jnp.concatenate(
        [r[start * size : (start + 1) * size, g * HD : (g + 1) * HD] for r in refs], axis=0
    )


def own_bias(tokens, rows):
    u = lax.broadcasted_iota(jnp.int32, (tokens, 4 * rows), 0)
    lane = lax.broadcasted_iota(jnp.int32, (tokens, 4 * rows), 1)
    return jnp.where((lane < rows) & (u <= lane % tokens), 0.0, MASKED)


def block_bias(info_ref, k, block):
    at = lax.broadcasted_iota(jnp.int32, (block, 1), 0)
    return jnp.where(at + info_ref[1 + k] * block < info_ref[0], 0.0, MASKED)


def with_own(blocks, own_ref, part, g):
    own = own_ref[part][:, g * HD : (g + 1) * HD]
    return jnp.concatenate([cols_of(blocks, part, g), own], axis=0)


def partial_stats(score, slope):
    top = jnp.max(score, axis=0, keepdims=True)
    e = jnp.exp2(score - top)
    total = jnp.sum(e, axis=0, keepdims=True)
    return top, total, jnp.sum(e * slope, axis=0, keepdims=True)


def add_bias(score, bias, own):
    at = bias.shape[0]
    return jnp.concatenate([score[:at] + bias, score[at:] + own], axis=0)


def join(one, two):
    top = jnp.maximum(one[0], two[0])
    f, h = jnp.exp2(one[0] - top), jnp.exp2(two[0] - top)
    return top, one[1] * f + two[1] * h, one[2] * f + two[2] * h


def pass_kernel(*refs):
    pass


def first_stats_kernel(to_log2, where, info_ref, *refs):
    qg, kvs, own_ref, out_ref = refs[0:4], refs[4:-3], refs[-3:-1], refs[-1]
    block = (kvs[0].shape[0] - 16) // 2
    groups = kvs[0].shape[1] // HD
    tokens = own_ref[0].shape[0]
    rows = qg[0].shape[1] // HD // groups * tokens
    bias = jnp.concatenate([block_bias(info_ref, k, block) for k in where], axis=0)
    own = own_bias(tokens, rows)
    out_ref[...] = jnp.zeros_like(out_ref)
    for g in range(groups):
        q, w = rows_of(qg, 0, g), rows_of(qg, 1, g)
        score = dot(with_own(kvs, own_ref, 0, g), q, NT) * to_log2
        slope = dot(with_own(kvs, own_ref, 1, g), w, NT)
        for i, value in enumerate(partial_stats(add_bias(score, bias, own), slope)):
            out_ref[i * groups + g : i * groups + g + 1, :] = value


def last_stats_kernel(to_log2, where, info_ref, *refs):
    qg, kvs, first_ref, out_ref = refs[0:4], refs[4:8], refs[8], refs[9]
    block = (kvs[0].shape[0] - 16) // 2
    groups = kvs[0].shape[1] // HD
    rows = qg[0].shape[1] // HD // groups * (qg[0].shape[0] // 2)
    bias = jnp.concatenate([block_bias(info_ref, k, block) for k in where], axis=0)
    out_ref[48:56, :] = sum(
        r[2 * block : 2 * block + 16, :HD].astype(jnp.float32)[:8] for r in kvs
    )
    for g in range(groups):
        q, w = rows_of(qg, 0, g), rows_of(qg, 1, g)
        blocks = [kvs[k] for k in where]
        score = dot(cols_of(blocks, 0, g), q, NT) * to_log2 + bias
        got = partial_stats(score, dot(cols_of(blocks, 1, g), w, NT))
        before = [first_ref[i * groups + g : i * groups + g + 1, :] for i in range(3)]
        got = join(before, got)
        for s in range(4):
            for i in range(3):
                at = 16 * i + 4 * s + g
                out_ref[at : at + 1, :] = got[i][:, s * rows : (s + 1) * rows]


def terms_kernel(to_log2, info_ref, *refs):
    qg, kvs, own_ref, score_out, slope_out = refs[0:4], refs[4:8], refs[8:10], refs[10], refs[11]
    block = (kvs[0].shape[0] - 16) // 2
    groups = kvs[0].shape[1] // HD
    tokens = own_ref[0].shape[0]
    rows = qg[0].shape[1] // HD // groups * tokens
    bias = jnp.concatenate([block_bias(info_ref, k, block) for k in range(4)], axis=0)
    own_rows = own_bias(tokens, rows)
    size = 4 * block + tokens
    for g in range(groups):
        at = slice(g * size, (g + 1) * size)
        score = dot(with_own(kvs, own_ref, 0, g), rows_of(qg, 0, g), NT) * to_log2
        score_out[at, :] = add_bias(score, bias, own_rows)
        slope_out[at, :] = dot(with_own(kvs, own_ref, 1, g), rows_of(qg, 1, g), NT)


def grads_kernel(*refs):
    qg, kvs, own_ref = refs[0:4], refs[4:8], refs[8:10]
    score_ref, slope_ref = refs[10:12]
    stats = refs[12:16]
    dq_own, dq_far, dq_sib, dkv_own = refs[16:20]
    dkv_out = refs[20:23]
    own_out, tot_out = refs[23:25]
    block = (kvs[0].shape[0] - 16) // 2
    groups = kvs[0].shape[1] // HD
    tokens = own_ref[0].shape[0]
    rows = qg[0].shape[1] // HD // groups * tokens
    size = 4 * block + tokens
    shifts, means = [], []
    for s in range(4):
        tops = [stats[e][(s ^ e) * 4 : (s ^ e) * 4 + 4, :] for e in range(4)]
        top = functools.reduce(jnp.maximum, tops)
        total, mixed = 0.0, 0.0
        for e in range(4):
            factor = jnp.exp2(tops[e] - top)
            at = (s ^ e) * 4
            total += stats[e][16 + at : 20 + at, :] * factor
            mixed += stats[e][32 + at : 36 + at, :] * factor
        shifts.append(top + jnp.log2(total))
        means.append(mixed / total)
    shift = jnp.concatenate(shifts, axis=1)
    mean = jnp.concatenate(means, axis=1)
    half = groups * block
    for i in range(tot_out.shape[0]):
        tot_out[i] = sum(stats[e][48:49, :] for e in range(4))
    for g in range(groups):
        q = rows_of(qg, 0, g)
        w = rows_of(qg, 1, g)
        k = with_own(kvs, own_ref, 0, g)
        sh, mn = shift[g : g + 1, :], mean[g : g + 1, :]
        span = slice(g * size, (g + 1) * size)
        p = jnp.exp2(score_ref[span, :] - sh)
        ds = (p * (slope_ref[span, :] - mn)).astype(jnp.bfloat16)
        dv = dot(p.astype(jnp.bfloat16), w, NN)
        dk = dot(ds, q, NN)
        dq = dot(k.T, ds, NN)
        own_cols = slice(g * HD, (g + 1) * HD)
        own_out[:tokens, own_cols] = dk[4 * block :]
        own_out[tokens:, own_cols] = dv[4 * block :]
        at = slice(g * HD, (g + 1) * HD)
        dq_own[at, :] = dq[:, :rows]
        dq_far[at, :] = dq[:, 2 * rows : 3 * rows]
        dq_sib[at, :] = dq[:, rows : 2 * rows].astype(jnp.bfloat16)
        dq_sib[half_at(dq_sib, g), :] = dq[:, 3 * rows :].astype(jnp.bfloat16)
        here = slice(g * block, (g + 1) * block)
        there = slice(half + g * block, half + (g + 1) * block)
        dkv_own[here, :] = dk[:block]
        dkv_own[there, :] = dv[:block]
        for e in range(3):
            part = slice((e + 1) * block, (e + 2) * block)
            dkv_out[e][here, :] = dk[part].astype(jnp.bfloat16)
            dkv_out[e][there, :] = dv[part].astype(jnp.bfloat16)


def half_at(ref, g):
    half = ref.shape[0] // 2
    return slice(half + g * HD, half + (g + 1) * HD)


def finish_kernel(loss_top, softmax_scale, *refs):
    dq_own, dq_core, dq_x, dkv_own, r1, r2, r3, own_ref, tot_ref = refs[:9]
    q_out, k_out, v_out, ok_out, ov_out = refs[9:]
    block = k_out.shape[0]
    groups = k_out.shape[1] // HD
    tokens = ok_out.shape[0]
    per_group = q_out.shape[1] // HD // groups
    half = groups * block
    f32 = jnp.float32
    count = functools.reduce(jnp.add, [tot_ref[i] for i in range(tot_ref.shape[0])])
    scale = loss_top / count[:1, :]
    key_scale = scale * softmax_scale
    for g in range(groups):
        cols = slice(g * HD, (g + 1) * HD)
        dq = (
            dq_own[cols, :]
            + dq_core[cols, :].astype(f32)
            + dq_x[cols, :].astype(f32)
        ).T * key_scale
        for x in range(per_group):
            h = g * per_group + x
            q_out[:, h * HD : (h + 1) * HD] = dq[x * tokens : (x + 1) * tokens].astype(
                jnp.bfloat16
            )
        for out, start, by in ((k_out, 0, key_scale), (v_out, half, scale)):
            at = slice(start + g * block, start + (g + 1) * block)
            term = (dkv_own[at, :] + r1[at, :].astype(f32)) + (
                r2[at, :].astype(f32) + r3[at, :].astype(f32)
            )
            out[:, cols] = (term * by).astype(jnp.bfloat16)
        ok_out[:, cols] = (own_ref[:tokens, cols] * key_scale).astype(jnp.bfloat16)
        ov_out[:, cols] = (own_ref[tokens:, cols] * scale).astype(jnp.bfloat16)


def per_device(
    queries,
    out_grad,
    advantage,
    comp_len,
    prefix_keys,
    prefix_values,
    own_keys,
    own_values,
    prompt_len,
):
    samples = lax.axis_size("sample")
    prompts = lax.axis_size("prompt")
    tokens, width = queries.shape[2], queries.shape[3]
    block, kv_width = prefix_keys.shape[1], prefix_keys.shape[2]
    groups = kv_width // HD
    softmax_scale = 1.0 / math.sqrt(HD)
    to_log2 = softmax_scale * math.log2(math.e)
    loss_top = prompts * samples * tokens * math.sqrt(block * samples) / 4.0
    bf16, f32 = jnp.bfloat16, jnp.float32
    vmem = pl.BlockSpec(memory_space=pltpu.VMEM)
    smem = pl.BlockSpec(memory_space=pltpu.SMEM)
    params = pltpu.CompilerParams(vmem_limit_bytes=VMEM_LIMIT)
    shape = jax.ShapeDtypeStruct

    def swap(array, mask):
        return lax.ppermute(array, "sample", [(i, i ^ mask) for i in range(samples)])

    at = lax.broadcasted_iota(jnp.int32, (2 * tokens, width), 0)
    weight = jnp.where(at - tokens < comp_len[0, 0], advantage[0, 0], 0.0)
    weight = jnp.where(at < tokens, 1.0, weight)
    qg0 = jnp.concatenate([queries[0, 0], out_grad[0, 0]], axis=0)
    qg0 = (qg0.astype(f32) * weight).astype(bf16)
    mark = jnp.broadcast_to(comp_len.astype(bf16), (16, kv_width))
    kv0 = jnp.concatenate([prefix_keys[0], prefix_values[0], mark], axis=0)
    own = [own_keys[0, 0], own_values[0, 0]]
    qg2 = swap(qg0, 8)
    kv = [kv0] + [swap(kv0, 2 * e) for e in (1, 2, 3)]
    kv[2], = pl.pallas_call(
        pass_kernel,
        out_shape=[shape(kv0.shape, bf16)] * 1,
        in_specs=[pl.BlockSpec(memory_space=pl.ANY)] * 1,
        out_specs=[pl.BlockSpec(memory_space=pl.ANY)] * 1,
        input_output_aliases={0: 0},
        cost_estimate=pl.CostEstimate(flops=20000000000, bytes_accessed=0, transcendentals=0),
        compiler_params=params,
        name="rows_here",
    )(kv[2])
    qg1 = swap(qg0, 1)
    qg3 = swap(qg2, 1)
    qg = [qg0, qg1, qg2, qg3]
    me = lax.axis_index("sample")
    info = jnp.stack([prompt_len[0]] + [me ^ (2 * e) for e in range(4)]).astype(jnp.int32)
    early, late = (0, 2), (1, 3)
    first = pl.pallas_call(
        functools.partial(first_stats_kernel, to_log2, early),
        out_shape=shape((16, width * 4 * tokens // HD // groups), f32),
        in_specs=[smem] + [vmem] * (6 + len(early)),
        out_specs=vmem,
        compiler_params=params,
        name="stats_first",
    )(info, *qg, *[kv[k] for k in early], *own)
    stats0 = pl.pallas_call(
        functools.partial(last_stats_kernel, to_log2, late),
        out_shape=shape((56, HD), f32),
        in_specs=[smem] + [vmem] * 9,
        out_specs=vmem,
        compiler_params=params,
        name="stats",
    )(info, *qg, *kv, first)
    stats = [stats0, swap(stats0, 1), swap(stats0, 8), swap(stats0, 9)]
    term_shape = shape((groups * (4 * block + tokens), width * 4 * tokens // HD // groups), f32)
    terms = pl.pallas_call(
        functools.partial(terms_kernel, to_log2),
        out_shape=[term_shape] * 2,
        in_specs=[smem] + [vmem] * 10,
        out_specs=[vmem] * 2,
        compiler_params=params,
        name="terms",
    )(info, *qg, *kv, *own)
    kv_rows = 2 * groups * block
    dq_rows = width // HD // 4 * HD
    outs = pl.pallas_call(
        grads_kernel,
        out_shape=[
            shape((dq_rows, HD), f32),
            shape((dq_rows, HD), f32),
            shape((2 * dq_rows, HD), bf16),
            shape((kv_rows, HD), f32),
        ]
        + [shape((kv_rows, HD), bf16)] * 3
        + [shape((2 * tokens, kv_width), f32), shape((prompts, 1, HD), f32)],
        in_specs=[vmem] * 16,
        out_specs=[vmem] * 9,
        compiler_params=params,
        name="grads",
    )(*qg, *kv, *own, *terms, *stats)
    dq_own, dq_far, dq_sib, dkv_own = outs[:4]
    dq_core = swap(dq_sib, 1)
    dq_x = swap((dq_far + dq_core[dq_rows:].astype(f32)).astype(bf16), 8)
    total = lax.all_to_all(outs[8], "prompt", 0, 0, tiled=True)
    received = [swap(outs[3 + e], 2 * e) for e in (1, 2, 3)]
    q_out, k_out, v_out, ok_out, ov_out = pl.pallas_call(
        functools.partial(finish_kernel, loss_top, softmax_scale),
        out_shape=[
            shape((tokens, width), bf16),
            shape((block, kv_width), bf16),
            shape((block, kv_width), bf16),
            shape((tokens, kv_width), bf16),
            shape((tokens, kv_width), bf16),
        ],
        in_specs=[vmem] * 9,
        out_specs=[vmem] * 5,
        compiler_params=params,
        name="finish",
    )(dq_own, dq_core, dq_x, dkv_own, *received, outs[7], total)
    return (q_out[None, None], k_out[None], v_out[None], ok_out[None, None], ov_out[None, None])


def solution(mesh):
    in_specs = (
        P("prompt", "sample", None, None),
        P("prompt", "sample", None, None),
        P("prompt", "sample"),
        P("prompt", "sample"),
        P("prompt", "sample", None),
        P("prompt", "sample", None),
        P("prompt", "sample", None, None),
        P("prompt", "sample", None, None),
        P("prompt"),
    )
    out_specs = (
        P("prompt", "sample", None, None),
        P("prompt", "sample", None),
        P("prompt", "sample", None),
        P("prompt", "sample", None, None),
        P("prompt", "sample", None, None),
    )
    return jax.shard_map(
        per_device, mesh=mesh, in_specs=in_specs, out_specs=out_specs, check_vma=False
    )
```

```python
import functools
import math

import jax
import jax.numpy as jnp
from jax import lax
from jax.experimental import pallas as pl
from jax.experimental.pallas import tpu as pltpu
from jax.sharding import PartitionSpec as P

HD = 128
MASKED = -1e30
VMEM_LIMIT = 24 * 1024 * 1024
NT = (((1,), (1,)), ((), ()))
NN = (((1,), (0,)), ((), ()))


def dot(a, b, dims):
    return lax.dot_general(a, b, dims, preferred_element_type=jnp.float32)


def rows_of(refs, kind, g):
    tokens = refs[0].shape[0] // 2
    rows = slice(kind * tokens, (kind + 1) * tokens)
    return jnp.concatenate(
        [r[rows, h * HD : (h + 1) * HD] for r in refs for h in range(4 * g, 4 * g + 4)], axis=0
    )


def cols_of(refs, start, g):
    size = (refs[0].shape[0] - 16) // 2
    return jnp.concatenate(
        [r[start * size : (start + 1) * size, g * HD : (g + 1) * HD] for r in refs], axis=0
    )


def own_bias(tokens, rows):
    u = lax.broadcasted_iota(jnp.int32, (tokens, 4 * rows), 0)
    lane = lax.broadcasted_iota(jnp.int32, (tokens, 4 * rows), 1)
    return jnp.where((lane < rows) & (u <= lane % tokens), 0.0, MASKED)


def block_bias(info_ref, k, block):
    at = lax.broadcasted_iota(jnp.int32, (block, 1), 0)
    return jnp.where(at + info_ref[1 + k] * block < info_ref[0], 0.0, MASKED)


def with_own(blocks, own_ref, part, g):
    own = own_ref[part][:, g * HD : (g + 1) * HD]
    return jnp.concatenate([cols_of(blocks, part, g), own], axis=0)


def partial_stats(score, slope):
    top = jnp.max(score, axis=0, keepdims=True)
    e = jnp.exp2(score - top)
    total = jnp.sum(e, axis=0, keepdims=True)
    return top, total, jnp.sum(e * slope, axis=0, keepdims=True)


def add_bias(score, bias, own):
    at = bias.shape[0]
    return jnp.concatenate([score[:at] + bias, score[at:] + own], axis=0)


def join(one, two):
    top = jnp.maximum(one[0], two[0])
    f, h = jnp.exp2(one[0] - top), jnp.exp2(two[0] - top)
    return top, one[1] * f + two[1] * h, one[2] * f + two[2] * h


def pass_kernel(*refs):
    pass


def first_stats_kernel(to_log2, where, info_ref, *refs):
    qg, kvs, own_ref, out_ref = refs[0:4], refs[4:-3], refs[-3:-1], refs[-1]
    block = (kvs[0].shape[0] - 16) // 2
    groups = kvs[0].shape[1] // HD
    tokens = own_ref[0].shape[0]
    rows = qg[0].shape[1] // HD // groups * tokens
    bias = jnp.concatenate([block_bias(info_ref, k, block) for k in where], axis=0)
    own = own_bias(tokens, rows)
    out_ref[...] = jnp.zeros_like(out_ref)
    for g in range(groups):
        q, w = rows_of(qg, 0, g), rows_of(qg, 1, g)
        score = dot(with_own(kvs, own_ref, 0, g), q, NT) * to_log2
        slope = dot(with_own(kvs, own_ref, 1, g), w, NT)
        for i, value in enumerate(partial_stats(add_bias(score, bias, own), slope)):
            out_ref[i * groups + g : i * groups + g + 1, :] = value


def last_stats_kernel(to_log2, where, info_ref, *refs):
    qg, kvs, first_ref, out_ref = refs[0:4], refs[4:8], refs[8], refs[9]
    block = (kvs[0].shape[0] - 16) // 2
    groups = kvs[0].shape[1] // HD
    rows = qg[0].shape[1] // HD // groups * (qg[0].shape[0] // 2)
    bias = jnp.concatenate([block_bias(info_ref, k, block) for k in where], axis=0)
    out_ref[48:56, :] = sum(
        r[2 * block : 2 * block + 16, :HD].astype(jnp.float32)[:8] for r in kvs
    )
    for g in range(groups):
        q, w = rows_of(qg, 0, g), rows_of(qg, 1, g)
        blocks = [kvs[k] for k in where]
        score = dot(cols_of(blocks, 0, g), q, NT) * to_log2 + bias
        got = partial_stats(score, dot(cols_of(blocks, 1, g), w, NT))
        before = [first_ref[i * groups + g : i * groups + g + 1, :] for i in range(3)]
        got = join(before, got)
        for s in range(4):
            for i in range(3):
                at = 16 * i + 4 * s + g
                out_ref[at : at + 1, :] = got[i][:, s * rows : (s + 1) * rows]


def terms_kernel(to_log2, info_ref, *refs):
    qg, kvs, own_ref, score_out, slope_out = refs[0:4], refs[4:8], refs[8:10], refs[10], refs[11]
    block = (kvs[0].shape[0] - 16) // 2
    groups = kvs[0].shape[1] // HD
    tokens = own_ref[0].shape[0]
    rows = qg[0].shape[1] // HD // groups * tokens
    bias = jnp.concatenate([block_bias(info_ref, k, block) for k in range(4)], axis=0)
    own_rows = own_bias(tokens, rows)
    size = 4 * block + tokens
    for g in range(groups):
        at = slice(g * size, (g + 1) * size)
        score = dot(with_own(kvs, own_ref, 0, g), rows_of(qg, 0, g), NT) * to_log2
        score_out[at, :] = add_bias(score, bias, own_rows)
        slope_out[at, :] = dot(with_own(kvs, own_ref, 1, g), rows_of(qg, 1, g), NT)


def grads_kernel(*refs):
    qg, kvs, own_ref = refs[0:4], refs[4:8], refs[8:10]
    score_ref, slope_ref = refs[10:12]
    stats = refs[12:16]
    dq_own, dq_far, dq_sib, dkv_own = refs[16:20]
    dkv_out = refs[20:23]
    own_out, tot_out = refs[23:25]
    block = (kvs[0].shape[0] - 16) // 2
    groups = kvs[0].shape[1] // HD
    tokens = own_ref[0].shape[0]
    rows = qg[0].shape[1] // HD // groups * tokens
    size = 4 * block + tokens
    peaks, logs, means = [], [], []
    for s in range(4):
        tops = [stats[e][(s ^ e) * 4 : (s ^ e) * 4 + 4, :] for e in range(4)]
        top = functools.reduce(jnp.maximum, tops)
        total, mixed = 0.0, 0.0
        for e in range(4):
            factor = jnp.exp2(tops[e] - top)
            at = (s ^ e) * 4
            total += stats[e][16 + at : 20 + at, :] * factor
            mixed += stats[e][32 + at : 36 + at, :] * factor
        peaks.append(top)
        logs.append(jnp.log2(total))
        means.append(mixed / total)
    peak = jnp.concatenate(peaks, axis=1)
    log = jnp.concatenate(logs, axis=1)
    mean = jnp.concatenate(means, axis=1)
    half = groups * block
    for i in range(tot_out.shape[0]):
        tot_out[i] = sum(stats[e][48:49, :] for e in range(4))
    for g in range(groups):
        q = rows_of(qg, 0, g)
        w = rows_of(qg, 1, g)
        k = with_own(kvs, own_ref, 0, g)
        pk, lg, mn = (x[g : g + 1, :] for x in (peak, log, mean))
        span = slice(g * size, (g + 1) * size)
        p = jnp.exp2((score_ref[span, :] - pk) - lg)
        ds = (p * (slope_ref[span, :] - mn)).astype(jnp.bfloat16)
        dv = dot(p.astype(jnp.bfloat16), w, NN)
        dk = dot(ds, q, NN)
        dq = dot(k.T, ds, NN)
        own_cols = slice(g * HD, (g + 1) * HD)
        own_out[:tokens, own_cols] = dk[4 * block :]
        own_out[tokens:, own_cols] = dv[4 * block :]
        at = slice(g * HD, (g + 1) * HD)
        dq_own[at, :] = dq[:, :rows]
        dq_far[at, :] = dq[:, 2 * rows : 3 * rows]
        dq_sib[at, :] = dq[:, rows : 2 * rows].astype(jnp.bfloat16)
        dq_sib[half_at(dq_sib, g), :] = dq[:, 3 * rows :].astype(jnp.bfloat16)
        here = slice(g * block, (g + 1) * block)
        there = slice(half + g * block, half + (g + 1) * block)
        dkv_own[here, :] = dk[:block]
        dkv_own[there, :] = dv[:block]
        for e in range(3):
            part = slice((e + 1) * block, (e + 2) * block)
            dkv_out[e][here, :] = dk[part].astype(jnp.bfloat16)
            dkv_out[e][there, :] = dv[part].astype(jnp.bfloat16)


def half_at(ref, g):
    half = ref.shape[0] // 2
    return slice(half + g * HD, half + (g + 1) * HD)


def finish_kernel(loss_top, softmax_scale, *refs):
    dq_own, dq_core, dq_x, dkv_own, r1, r2, r3, own_ref, tot_ref = refs[:9]
    q_out, k_out, v_out, ok_out, ov_out = refs[9:]
    block = k_out.shape[0]
    groups = k_out.shape[1] // HD
    tokens = ok_out.shape[0]
    per_group = q_out.shape[1] // HD // groups
    half = groups * block
    f32 = jnp.float32
    count = functools.reduce(jnp.add, [tot_ref[i] for i in range(tot_ref.shape[0])])
    scale = loss_top / count[:1, :]
    key_scale = scale * softmax_scale
    for g in range(groups):
        cols = slice(g * HD, (g + 1) * HD)
        dq = (
            dq_own[cols, :]
            + dq_core[cols, :].astype(f32)
            + dq_x[cols, :].astype(f32)
        ).T * key_scale
        for x in range(per_group):
            h = g * per_group + x
            q_out[:, h * HD : (h + 1) * HD] = dq[x * tokens : (x + 1) * tokens].astype(
                jnp.bfloat16
            )
        for out, start, by in ((k_out, 0, key_scale), (v_out, half, scale)):
            at = slice(start + g * block, start + (g + 1) * block)
            term = (dkv_own[at, :] + r1[at, :].astype(f32)) + (
                r2[at, :].astype(f32) + r3[at, :].astype(f32)
            )
            out[:, cols] = (term * by).astype(jnp.bfloat16)
        ok_out[:, cols] = (own_ref[:tokens, cols] * key_scale).astype(jnp.bfloat16)
        ov_out[:, cols] = (own_ref[tokens:, cols] * scale).astype(jnp.bfloat16)


def per_device(
    queries,
    out_grad,
    advantage,
    comp_len,
    prefix_keys,
    prefix_values,
    own_keys,
    own_values,
    prompt_len,
):
    samples = lax.axis_size("sample")
    prompts = lax.axis_size("prompt")
    tokens, width = queries.shape[2], queries.shape[3]
    block, kv_width = prefix_keys.shape[1], prefix_keys.shape[2]
    groups = kv_width // HD
    softmax_scale = 1.0 / math.sqrt(HD)
    to_log2 = softmax_scale * math.log2(math.e)
    loss_top = prompts * samples * tokens * math.sqrt(block * samples) / 4.0
    bf16, f32 = jnp.bfloat16, jnp.float32
    vmem = pl.BlockSpec(memory_space=pltpu.VMEM)
    smem = pl.BlockSpec(memory_space=pltpu.SMEM)
    params = pltpu.CompilerParams(vmem_limit_bytes=VMEM_LIMIT)
    shape = jax.ShapeDtypeStruct

    def swap(array, mask):
        return lax.ppermute(array, "sample", [(i, i ^ mask) for i in range(samples)])

    at = lax.broadcasted_iota(jnp.int32, (2 * tokens, width), 0)
    weight = jnp.where(at - tokens < comp_len[0, 0], advantage[0, 0], 0.0)
    weight = jnp.where(at < tokens, 1.0, weight)
    qg0 = jnp.concatenate([queries[0, 0], out_grad[0, 0]], axis=0)
    qg0 = (qg0.astype(f32) * weight).astype(bf16)
    mark = jnp.broadcast_to(comp_len.astype(bf16), (16, kv_width))
    kv0 = jnp.concatenate([prefix_keys[0], prefix_values[0], mark], axis=0)
    own = [own_keys[0, 0], own_values[0, 0]]
    qg2 = swap(qg0, 8)
    kv = [kv0] + [swap(kv0, 2 * e) for e in (1, 2, 3)]
    kv[2], = pl.pallas_call(
        pass_kernel,
        out_shape=[shape(kv0.shape, bf16)] * 1,
        in_specs=[pl.BlockSpec(memory_space=pl.ANY)] * 1,
        out_specs=[pl.BlockSpec(memory_space=pl.ANY)] * 1,
        input_output_aliases={0: 0},
        cost_estimate=pl.CostEstimate(flops=20000000000, bytes_accessed=0, transcendentals=0),
        compiler_params=params,
        name="rows_here",
    )(kv[2])
    qg1 = swap(qg0, 1)
    qg3 = swap(qg2, 1)
    qg = [qg0, qg1, qg2, qg3]
    me = lax.axis_index("sample")
    info = jnp.stack([prompt_len[0]] + [me ^ (2 * e) for e in range(4)]).astype(jnp.int32)
    early, late = (0, 2), (1, 3)
    first = pl.pallas_call(
        functools.partial(first_stats_kernel, to_log2, early),
        out_shape=shape((16, width * 4 * tokens // HD // groups), f32),
        in_specs=[smem] + [vmem] * (6 + len(early)),
        out_specs=vmem,
        compiler_params=params,
        name="stats_first",
    )(info, *qg, *[kv[k] for k in early], *own)
    stats0 = pl.pallas_call(
        functools.partial(last_stats_kernel, to_log2, late),
        out_shape=shape((56, HD), f32),
        in_specs=[smem] + [vmem] * 9,
        out_specs=vmem,
        compiler_params=params,
        name="stats",
    )(info, *qg, *kv, first)
    stats = [stats0, swap(stats0, 1), swap(stats0, 8), swap(stats0, 9)]
    term_shape = shape((groups * (4 * block + tokens), width * 4 * tokens // HD // groups), f32)
    terms = pl.pallas_call(
        functools.partial(terms_kernel, to_log2),
        out_shape=[term_shape] * 2,
        in_specs=[smem] + [vmem] * 10,
        out_specs=[vmem] * 2,
        compiler_params=params,
        name="terms",
    )(info, *qg, *kv, *own)
    kv_rows = 2 * groups * block
    dq_rows = width // HD // 4 * HD
    outs = pl.pallas_call(
        grads_kernel,
        out_shape=[
            shape((dq_rows, HD), f32),
            shape((dq_rows, HD), f32),
            shape((2 * dq_rows, HD), bf16),
            shape((kv_rows, HD), f32),
        ]
        + [shape((kv_rows, HD), bf16)] * 3
        + [shape((2 * tokens, kv_width), f32), shape((prompts, 1, HD), f32)],
        in_specs=[vmem] * 16,
        out_specs=[vmem] * 9,
        compiler_params=params,
        name="grads",
    )(*qg, *kv, *own, *terms, *stats)
    dq_own, dq_far, dq_sib, dkv_own = outs[:4]
    dq_core = swap(dq_sib, 1)
    dq_x = swap((dq_far + dq_core[dq_rows:].astype(f32)).astype(bf16), 8)
    total = lax.all_to_all(outs[8], "prompt", 0, 0, tiled=True)
    received = [swap(outs[3 + e], 2 * e) for e in (1, 2, 3)]
    q_out, k_out, v_out, ok_out, ov_out = pl.pallas_call(
        functools.partial(finish_kernel, loss_top, softmax_scale),
        out_shape=[
            shape((tokens, width), bf16),
            shape((block, kv_width), bf16),
            shape((block, kv_width), bf16),
            shape((tokens, kv_width), bf16),
            shape((tokens, kv_width), bf16),
        ],
        in_specs=[vmem] * 9,
        out_specs=[vmem] * 5,
        compiler_params=params,
        name="finish",
    )(dq_own, dq_core, dq_x, dkv_own, *received, outs[7], total)
    return (q_out[None, None], k_out[None], v_out[None], ok_out[None, None], ov_out[None, None])


def solution(mesh):
    in_specs = (
        P("prompt", "sample", None, None),
        P("prompt", "sample", None, None),
        P("prompt", "sample"),
        P("prompt", "sample"),
        P("prompt", "sample", None),
        P("prompt", "sample", None),
        P("prompt", "sample", None, None),
        P("prompt", "sample", None, None),
        P("prompt"),
    )
    out_specs = (
        P("prompt", "sample", None, None),
        P("prompt", "sample", None),
        P("prompt", "sample", None),
        P("prompt", "sample", None, None),
        P("prompt", "sample", None, None),
    )
    return jax.shard_map(
        per_device, mesh=mesh, in_specs=in_specs, out_specs=out_specs, check_vma=False
    )
```

```python
import functools
import math

import jax
import jax.numpy as jnp
from jax import lax
from jax.experimental import pallas as pl
from jax.experimental.pallas import tpu as pltpu
from jax.sharding import PartitionSpec as P

HD = 128
MASKED = -1e30
VMEM_LIMIT = 24 * 1024 * 1024
NT = (((1,), (1,)), ((), ()))
NN = (((1,), (0,)), ((), ()))


def dot(a, b, dims):
    return lax.dot_general(a, b, dims, preferred_element_type=jnp.float32)


def rows_of(refs, kind, g):
    tokens = refs[0].shape[0] // 2
    rows = slice(kind * tokens, (kind + 1) * tokens)
    return jnp.concatenate(
        [r[rows, h * HD : (h + 1) * HD] for r in refs for h in range(4 * g, 4 * g + 4)], axis=0
    )


def cols_of(refs, start, g):
    size = (refs[0].shape[0] - 16) // 2
    return jnp.concatenate(
        [r[start * size : (start + 1) * size, g * HD : (g + 1) * HD] for r in refs], axis=0
    )


def own_bias(tokens, rows):
    u = lax.broadcasted_iota(jnp.int32, (tokens, 4 * rows), 0)
    lane = lax.broadcasted_iota(jnp.int32, (tokens, 4 * rows), 1)
    return jnp.where((lane < rows) & (u <= lane % tokens), 0.0, MASKED)


def block_bias(info_ref, k, block):
    at = lax.broadcasted_iota(jnp.int32, (block, 1), 0)
    return jnp.where(at + info_ref[1 + k] * block < info_ref[0], 0.0, MASKED)


def with_own(blocks, own_ref, part, g):
    own = own_ref[part][:, g * HD : (g + 1) * HD]
    return jnp.concatenate([cols_of(blocks, part, g), own], axis=0)


def partial_stats(score, slope):
    top = jnp.max(score, axis=0, keepdims=True)
    e = jnp.exp2(score - top)
    total = jnp.sum(e, axis=0, keepdims=True)
    return top, total, jnp.sum(e * slope, axis=0, keepdims=True)


def add_bias(score, bias, own):
    at = bias.shape[0]
    return jnp.concatenate([score[:at] + bias, score[at:] + own], axis=0)


def join(one, two):
    top = jnp.maximum(one[0], two[0])
    f, h = jnp.exp2(one[0] - top), jnp.exp2(two[0] - top)
    return top, one[1] * f + two[1] * h, one[2] * f + two[2] * h


def pass_kernel(*refs):
    pass


def first_stats_kernel(to_log2, where, info_ref, *refs):
    qg, kvs, own_ref, out_ref = refs[0:4], refs[4:-3], refs[-3:-1], refs[-1]
    block = (kvs[0].shape[0] - 16) // 2
    groups = kvs[0].shape[1] // HD
    tokens = own_ref[0].shape[0]
    rows = qg[0].shape[1] // HD // groups * tokens
    bias = jnp.concatenate([block_bias(info_ref, k, block) for k in where], axis=0)
    own = own_bias(tokens, rows)
    out_ref[...] = jnp.zeros_like(out_ref)
    for g in range(groups):
        q, w = rows_of(qg, 0, g), rows_of(qg, 1, g)
        score = dot(with_own(kvs, own_ref, 0, g), q, NT) * to_log2
        slope = dot(with_own(kvs, own_ref, 1, g), w, NT)
        for i, value in enumerate(partial_stats(add_bias(score, bias, own), slope)):
            out_ref[i * groups + g : i * groups + g + 1, :] = value


def last_stats_kernel(to_log2, where, info_ref, *refs):
    qg, kvs, first_ref, out_ref = refs[0:4], refs[4:8], refs[8], refs[9]
    block = (kvs[0].shape[0] - 16) // 2
    groups = kvs[0].shape[1] // HD
    rows = qg[0].shape[1] // HD // groups * (qg[0].shape[0] // 2)
    bias = jnp.concatenate([block_bias(info_ref, k, block) for k in where], axis=0)
    out_ref[48:56, :] = sum(
        r[2 * block : 2 * block + 16, :HD].astype(jnp.float32)[:8] for r in kvs
    )
    for g in range(groups):
        q, w = rows_of(qg, 0, g), rows_of(qg, 1, g)
        blocks = [kvs[k] for k in where]
        score = dot(cols_of(blocks, 0, g), q, NT) * to_log2 + bias
        got = partial_stats(score, dot(cols_of(blocks, 1, g), w, NT))
        before = [first_ref[i * groups + g : i * groups + g + 1, :] for i in range(3)]
        got = join(before, got)
        for s in range(4):
            for i in range(3):
                at = 16 * i + 4 * s + g
                out_ref[at : at + 1, :] = got[i][:, s * rows : (s + 1) * rows]


def terms_kernel(to_log2, info_ref, *refs):
    qg, kvs, own_ref, score_out, slope_out = refs[0:4], refs[4:8], refs[8:10], refs[10], refs[11]
    block = (kvs[0].shape[0] - 16) // 2
    groups = kvs[0].shape[1] // HD
    tokens = own_ref[0].shape[0]
    rows = qg[0].shape[1] // HD // groups * tokens
    bias = jnp.concatenate([block_bias(info_ref, k, block) for k in range(4)], axis=0)
    own_rows = own_bias(tokens, rows)
    size = 4 * block + tokens
    for g in range(groups):
        at = slice(g * size, (g + 1) * size)
        score = dot(with_own(kvs, own_ref, 0, g), rows_of(qg, 0, g), NT) * to_log2
        score_out[at, :] = add_bias(score, bias, own_rows)
        slope_out[at, :] = dot(with_own(kvs, own_ref, 1, g), rows_of(qg, 1, g), NT)


def grads_kernel(*refs):
    qg, kvs, own_ref = refs[0:4], refs[4:8], refs[8:10]
    score_ref, slope_ref = refs[10:12]
    stats = refs[12:16]
    dq_own, dq_far, dq_sib, dkv_own = refs[16:20]
    dkv_out = refs[20:23]
    own_out, tot_out = refs[23:25]
    block = (kvs[0].shape[0] - 16) // 2
    groups = kvs[0].shape[1] // HD
    tokens = own_ref[0].shape[0]
    rows = qg[0].shape[1] // HD // groups * tokens
    size = 4 * block + tokens
    peaks, logs, means = [], [], []
    for s in range(4):
        tops = [stats[e][(s ^ e) * 4 : (s ^ e) * 4 + 4, :] for e in range(4)]
        top = functools.reduce(jnp.maximum, tops)
        total, mixed = 0.0, 0.0
        for e in range(4):
            factor = jnp.exp2(tops[e] - top)
            at = (s ^ e) * 4
            total += stats[e][16 + at : 20 + at, :] * factor
            mixed += stats[e][32 + at : 36 + at, :] * factor
        peaks.append(top)
        logs.append(jnp.log2(total))
        means.append(mixed / total)
    peak = jnp.concatenate(peaks, axis=1)
    log = jnp.concatenate(logs, axis=1)
    mean = jnp.concatenate(means, axis=1)
    half = groups * block
    for i in range(tot_out.shape[0]):
        tot_out[i] = sum(stats[e][48:49, :1] for e in range(4))
    for g in range(groups):
        q = rows_of(qg, 0, g)
        w = rows_of(qg, 1, g)
        k = with_own(kvs, own_ref, 0, g)
        pk, lg, mn = (x[g : g + 1, :] for x in (peak, log, mean))
        span = slice(g * size, (g + 1) * size)
        p = jnp.exp2((score_ref[span, :] - pk) - lg)
        ds = (p * (slope_ref[span, :] - mn)).astype(jnp.bfloat16)
        dv = dot(p.astype(jnp.bfloat16), w, NN)
        dk = dot(ds, q, NN)
        dq = dot(k.T, ds, NN)
        own_cols = slice(g * HD, (g + 1) * HD)
        own_out[:tokens, own_cols] = dk[4 * block :]
        own_out[tokens:, own_cols] = dv[4 * block :]
        at = slice(g * HD, (g + 1) * HD)
        dq_own[at, :] = dq[:, :rows]
        dq_far[at, :] = dq[:, 2 * rows : 3 * rows]
        dq_sib[at, :] = dq[:, rows : 2 * rows].astype(jnp.bfloat16)
        dq_sib[half_at(dq_sib, g), :] = dq[:, 3 * rows :].astype(jnp.bfloat16)
        here = slice(g * block, (g + 1) * block)
        there = slice(half + g * block, half + (g + 1) * block)
        dkv_own[here, :] = dk[:block]
        dkv_own[there, :] = dv[:block]
        for e in range(3):
            part = slice((e + 1) * block, (e + 2) * block)
            dkv_out[e][here, :] = dk[part].astype(jnp.bfloat16)
            dkv_out[e][there, :] = dv[part].astype(jnp.bfloat16)


def half_at(ref, g):
    half = ref.shape[0] // 2
    return slice(half + g * HD, half + (g + 1) * HD)


def finish_kernel(loss_top, softmax_scale, *refs):
    dq_own, dq_core, dq_x, dkv_own, r1, r2, r3, own_ref, tot_ref = refs[:9]
    q_out, k_out, v_out, ok_out, ov_out = refs[9:]
    block = k_out.shape[0]
    groups = k_out.shape[1] // HD
    tokens = ok_out.shape[0]
    per_group = q_out.shape[1] // HD // groups
    half = groups * block
    f32 = jnp.float32
    count = functools.reduce(jnp.add, [tot_ref[i] for i in range(tot_ref.shape[0])])
    scale = loss_top / count[:1, :]
    key_scale = scale * softmax_scale
    for g in range(groups):
        cols = slice(g * HD, (g + 1) * HD)
        dq = (
            dq_own[cols, :]
            + dq_core[cols, :].astype(f32)
            + dq_x[cols, :].astype(f32)
        ).T * key_scale
        for x in range(per_group):
            h = g * per_group + x
            q_out[:, h * HD : (h + 1) * HD] = dq[x * tokens : (x + 1) * tokens].astype(
                jnp.bfloat16
            )
        for out, start, by in ((k_out, 0, key_scale), (v_out, half, scale)):
            at = slice(start + g * block, start + (g + 1) * block)
            term = (dkv_own[at, :] + r1[at, :].astype(f32)) + (
                r2[at, :].astype(f32) + r3[at, :].astype(f32)
            )
            out[:, cols] = (term * by).astype(jnp.bfloat16)
        ok_out[:, cols] = (own_ref[:tokens, cols] * key_scale).astype(jnp.bfloat16)
        ov_out[:, cols] = (own_ref[tokens:, cols] * scale).astype(jnp.bfloat16)


def per_device(
    queries,
    out_grad,
    advantage,
    comp_len,
    prefix_keys,
    prefix_values,
    own_keys,
    own_values,
    prompt_len,
):
    samples = lax.axis_size("sample")
    prompts = lax.axis_size("prompt")
    tokens, width = queries.shape[2], queries.shape[3]
    block, kv_width = prefix_keys.shape[1], prefix_keys.shape[2]
    groups = kv_width // HD
    softmax_scale = 1.0 / math.sqrt(HD)
    to_log2 = softmax_scale * math.log2(math.e)
    loss_top = prompts * samples * tokens * math.sqrt(block * samples) / 4.0
    bf16, f32 = jnp.bfloat16, jnp.float32
    vmem = pl.BlockSpec(memory_space=pltpu.VMEM)
    smem = pl.BlockSpec(memory_space=pltpu.SMEM)
    params = pltpu.CompilerParams(vmem_limit_bytes=VMEM_LIMIT)
    shape = jax.ShapeDtypeStruct

    def swap(array, mask):
        return lax.ppermute(array, "sample", [(i, i ^ mask) for i in range(samples)])

    at = lax.broadcasted_iota(jnp.int32, (2 * tokens, width), 0)
    weight = jnp.where(at - tokens < comp_len[0, 0], advantage[0, 0], 0.0)
    weight = jnp.where(at < tokens, 1.0, weight)
    qg0 = jnp.concatenate([queries[0, 0], out_grad[0, 0]], axis=0)
    qg0 = (qg0.astype(f32) * weight).astype(bf16)
    mark = jnp.broadcast_to(comp_len.astype(bf16), (16, kv_width))
    kv0 = jnp.concatenate([prefix_keys[0], prefix_values[0], mark], axis=0)
    own = [own_keys[0, 0], own_values[0, 0]]
    qg2 = swap(qg0, 8)
    kv = [kv0] + [swap(kv0, 2 * e) for e in (1, 2, 3)]
    kv[2], = pl.pallas_call(
        pass_kernel,
        out_shape=[shape(kv0.shape, bf16)] * 1,
        in_specs=[pl.BlockSpec(memory_space=pl.ANY)] * 1,
        out_specs=[pl.BlockSpec(memory_space=pl.ANY)] * 1,
        input_output_aliases={0: 0},
        cost_estimate=pl.CostEstimate(flops=20000000000, bytes_accessed=0, transcendentals=0),
        compiler_params=params,
        name="rows_here",
    )(kv[2])
    qg1 = swap(qg0, 1)
    qg3 = swap(qg2, 1)
    qg = [qg0, qg1, qg2, qg3]
    me = lax.axis_index("sample")
    info = jnp.stack([prompt_len[0]] + [me ^ (2 * e) for e in range(4)]).astype(jnp.int32)
    early, late = (0, 2), (1, 3)
    first = pl.pallas_call(
        functools.partial(first_stats_kernel, to_log2, early),
        out_shape=shape((16, width * 4 * tokens // HD // groups), f32),
        in_specs=[smem] + [vmem] * (6 + len(early)),
        out_specs=vmem,
        compiler_params=params,
        name="stats_first",
    )(info, *qg, *[kv[k] for k in early], *own)
    stats0 = pl.pallas_call(
        functools.partial(last_stats_kernel, to_log2, late),
        out_shape=shape((56, HD), f32),
        in_specs=[smem] + [vmem] * 9,
        out_specs=vmem,
        compiler_params=params,
        name="stats",
    )(info, *qg, *kv, first)
    stats = [stats0, swap(stats0, 1), swap(stats0, 8), swap(stats0, 9)]
    term_shape = shape((groups * (4 * block + tokens), width * 4 * tokens // HD // groups), f32)
    terms = pl.pallas_call(
        functools.partial(terms_kernel, to_log2),
        out_shape=[term_shape] * 2,
        in_specs=[smem] + [vmem] * 10,
        out_specs=[vmem] * 2,
        compiler_params=params,
        name="terms",
    )(info, *qg, *kv, *own)
    kv_rows = 2 * groups * block
    dq_rows = width // HD // 4 * HD
    outs = pl.pallas_call(
        grads_kernel,
        out_shape=[
            shape((dq_rows, HD), f32),
            shape((dq_rows, HD), f32),
            shape((2 * dq_rows, HD), bf16),
            shape((kv_rows, HD), f32),
        ]
        + [shape((kv_rows, HD), bf16)] * 3
        + [shape((2 * tokens, kv_width), f32), shape((prompts, 1, 1), f32)],
        in_specs=[vmem] * 16,
        out_specs=[vmem] * 9,
        compiler_params=params,
        name="grads",
    )(*qg, *kv, *own, *terms, *stats)
    dq_own, dq_far, dq_sib, dkv_own = outs[:4]
    dq_core = swap(dq_sib, 1)
    dq_x = swap((dq_far + dq_core[dq_rows:].astype(f32)).astype(bf16), 8)
    total = lax.all_to_all(outs[8], "prompt", 0, 0, tiled=True)
    received = [swap(outs[3 + e], 2 * e) for e in (1, 2, 3)]
    q_out, k_out, v_out, ok_out, ov_out = pl.pallas_call(
        functools.partial(finish_kernel, loss_top, softmax_scale),
        out_shape=[
            shape((tokens, width), bf16),
            shape((block, kv_width), bf16),
            shape((block, kv_width), bf16),
            shape((tokens, kv_width), bf16),
            shape((tokens, kv_width), bf16),
        ],
        in_specs=[vmem] * 9,
        out_specs=[vmem] * 5,
        compiler_params=params,
        name="finish",
    )(dq_own, dq_core, dq_x, dkv_own, *received, outs[7], total)
    return (q_out[None, None], k_out[None], v_out[None], ok_out[None, None], ov_out[None, None])


def solution(mesh):
    in_specs = (
        P("prompt", "sample", None, None),
        P("prompt", "sample", None, None),
        P("prompt", "sample"),
        P("prompt", "sample"),
        P("prompt", "sample", None),
        P("prompt", "sample", None),
        P("prompt", "sample", None, None),
        P("prompt", "sample", None, None),
        P("prompt"),
    )
    out_specs = (
        P("prompt", "sample", None, None),
        P("prompt", "sample", None),
        P("prompt", "sample", None),
        P("prompt", "sample", None, None),
        P("prompt", "sample", None, None),
    )
    return jax.shard_map(
        per_device, mesh=mesh, in_specs=in_specs, out_specs=out_specs, check_vma=False
    )
```
